32 devices in a mesh: context: 2 (over x), tensor: 4 (over z), dp: 4 (over y, core).
Axes of the slice: x: 2, y: 2, z: 4, core: 2. Of those that a mesh axis runs over, the one named last changes fastest.
Arguments:
- grad_out: bfloat16 [4, 512, 1024], P('dp', 'context', 'tensor'), may hold values from -6 to 6
- inputs: bfloat16 [4, 512, 1024], P('dp', 'context', 'tensor'), may hold values from -0.125 to 0.125
- filt: bfloat16 [512, 1024], P('context', 'tensor'), may hold values from -0.25 to 0.25
Outputs:
- input_grad: bfloat16 [4, 512, 1024], P('dp', 'context', 'tensor')
- filter_grad: float32 [512, 1024], P('context', 'tensor')
The draws below stay inside these ranges and needn't reach their ends.
All inputs are finite; a program needn't handle non-finite values.
Results may differ from the reference program's by a relative error of at most 0.001.
Values may be sent and summed in bfloat16 or wider, within the bound.
A program may use at most 64 MiB of HBM per device.

```python
import jax
import jax.numpy as jnp

CHANNELS = 1024
SEQ = 512
BATCH = 4


def level_of(stream_key, dims, cuts, low, high):
    def one(dim, blocks):
        steps = jax.random.uniform(jax.random.fold_in(jax.random.fold_in(stream_key, 6), dim), (blocks,), jnp.float32, low / len(cuts), high / len(cuts))
        return jnp.repeat(jnp.exp(steps), dims[dim] // blocks).reshape((-1,) + (1,) * (len(dims) - dim - 1))

    factor_of = one(*cuts[0])
    for cut in cuts[1:]:
        factor_of = factor_of * one(*cut)
    return factor_of


def gaussian(stream_key, dims, deviation, most, pieces=(), dtype=jnp.bfloat16):
    loudness = level_of(stream_key, dims, pieces, -0.22, 0.18) if pieces else 1.0
    values = jax.random.normal(stream_key, dims, jnp.float32) * deviation * loudness
    return jnp.minimum(jnp.maximum(values, -most), most).astype(dtype)


def setup_inputs(seed: int = 0) -> dict:
    key_list = jax.random.split(jax.random.key(seed), 4)
    grad_out = gaussian(key_list[0], (BATCH, SEQ, CHANNELS), 1.0, 6.0, ((0, 4), (1, 2), (2, 4)))
    inputs = gaussian(key_list[1], (BATCH, SEQ, CHANNELS), (BATCH * SEQ) ** -0.5, 0.125, ((0, 4), (1, 2), (2, 4)))
    filt = gaussian(key_list[2], (SEQ, CHANNELS), SEQ ** -0.5, 0.25, ((0, 2), (1, 4)))
    return {"grad_out": grad_out, "inputs": inputs, "filt": filt}


def reference(grad_out, inputs, filt):
    padded_length = 2 * grad_out.shape[1]
    spec_grad = jnp.fft.rfft(grad_out.astype(jnp.float32), n=padded_length, axis=1)
    spec_input = jnp.fft.rfft(inputs.astype(jnp.float32), n=padded_length, axis=1)
    spec_filter = jnp.fft.rfft(filt.astype(jnp.float32), n=padded_length, axis=0)
    input_grad = jnp.fft.irfft(spec_grad * jnp.conj(spec_filter)[None], n=padded_length, axis=1)[:, :SEQ]
    summed = jnp.sum(spec_grad * jnp.conj(spec_input), axis=0)
    filter_grad = jnp.fft.irfft(summed, n=padded_length, axis=0)[:SEQ]
    return input_grad.astype(jnp.bfloat16), filter_grad.astype(jnp.float32)
```

```python
import functools
import math

import jax
import jax.numpy as jnp
import ml_dtypes
import numpy as np
from jax import lax
from jax.experimental import pallas as pl
from jax.experimental.pallas import tpu as pltpu
from jax.sharding import PartitionSpec as P

MESH = pl.DeviceIdType.MESH
NT = (((1,), (1,)), ((), ()))


def half_step_table(n):
    k = np.concatenate([np.arange(0, n, 2), np.arange(1, n, 2)])
    turns = (np.arange(n)[:, None] * (2 * k[None, :] + 1)) % (4 * n)
    angle = turns * (math.pi / (2 * n))
    table = np.concatenate([np.cos(angle), -np.sin(angle)], axis=1)
    high = table.astype(ml_dtypes.bfloat16)
    low = (table - high.astype(np.float64)).astype(ml_dtypes.bfloat16)
    return high, low


def dot(a, b):
    return jnp.dot(a, b, preferred_element_type=jnp.float32)


def dot_nt(a, b):
    return lax.dot_general(a, b, NT, preferred_element_type=jnp.float32)


def corr(fr, fi, gr, gi):
    return fr * gr + fi * gi, fr * gi - fi * gr


def kernel(
    n_ctx, n_dp,
    g_hbm, x_hbm, f_hbm, wh_hbm, wl_hbm,
    dx_ref, h_ref,
    g_in, x_in, f_in, wh, wl,
    out1, outf, in1, inf, spec, specf, s_hi, s_lo, h_out, dx_out, h_in, dx_in,
    load_sem, send1, recv1, sendf, recvf, send_h, recv_h, send_dx, recv_dx,
):
    n, width = g_hbm.shape
    group = n_ctx * n_dp
    cb = width // group
    half_lanes = n // 2
    ctx = lax.axis_index("context")
    dp = lax.axis_index("dp")
    me = ctx * n_dp + dp

    barrier = pltpu.get_barrier_semaphore()
    offsets = [(dc, dd) for dc in range(n_ctx - 1, -1, -1) for dd in range(n_dp - 1, -1, -1)]
    remote = [o for o in offsets if o != (0, 0)]

    def ahead(dc, dd):
        return lax.rem(ctx + dc, n_ctx), lax.rem(dp + dd, n_dp)

    def behind(dc, dd):
        return lax.rem(ctx + n_ctx - dc, n_ctx), lax.rem(dp + n_dp - dd, n_dp)

    for o in remote:
        pc, pd = ahead(*o)
        pl.semaphore_signal(barrier, inc=1, device_id={"context": pc, "dp": pd}, device_id_type=MESH)
    loads = [
        pltpu.make_async_copy(src, dst, load_sem.at[i])
        for i, (src, dst) in enumerate(
            [(g_hbm, g_in), (x_hbm, x_in), (f_hbm, f_in), (wh_hbm, wh), (wl_hbm, wl)]
        )
    ]
    for c in loads:
        c.start()
    loads[0].wait()
    out1[:, 0] = g_in[...].T.reshape(group, cb, n)
    loads[1].wait()
    out1[:, 1] = x_in[...].T.reshape(group, cb, n)
    loads[2].wait()
    outf[...] = f_in[...].T.reshape(group, cb, n)
    pl.semaphore_wait(barrier, group - 1)

    def to_peer(o):
        pc, pd = ahead(*o)
        peer = pc * n_dp + pd
        return pltpu.make_async_remote_copy(
            src_ref=out1.at[peer], dst_ref=in1.at[ctx, dp],
            send_sem=send1.at[peer], recv_sem=recv1.at[me],
            device_id={"context": pc, "dp": pd}, device_id_type=MESH,
        )

    sent = [to_peer(o) for o in remote]
    for c in sent:
        c.start()
    for dc in range(1, n_ctx):
        pc, _ = ahead(dc, 0)
        c = pltpu.make_async_remote_copy(
            src_ref=outf.at[pc * n_dp + dp], dst_ref=inf.at[ctx],
            send_sem=sendf.at[dc], recv_sem=recvf.at[ctx],
            device_id={"context": pc, "dp": dp}, device_id_type=MESH,
        )
        c.start()
        sent.append(c)
    in1[ctx, dp] = out1[me]
    inf[ctx] = outf[me]
    loads[3].wait()
    loads[4].wait()
    for o in remote:
        sc, sd = behind(*o)
        pltpu.make_async_remote_copy(
            src_ref=out1.at[me], dst_ref=in1.at[sc, sd],
            send_sem=send1.at[me], recv_sem=recv1.at[sc * n_dp + sd],
            device_id={"context": sc, "dp": sd}, device_id_type=MESH,
        ).wait_recv()
    for dc in range(1, n_ctx):
        sc, _ = behind(dc, 0)
        pltpu.make_async_remote_copy(
            src_ref=outf.at[me], dst_ref=inf.at[sc],
            send_sem=sendf.at[0], recv_sem=recvf.at[sc],
            device_id={"context": sc, "dp": dp}, device_id_type=MESH,
        ).wait_recv()

    rows = in1[...].reshape(group * 2 * cb, n)
    spec[...] = (dot(rows, wh[...]) + dot(rows, wl[...])).reshape(spec.shape)
    rows_f = inf[...].reshape(n_ctx * cb, n)
    specf[...] = (dot(rows_f, wh[...]) + dot(rows_f, wl[...])).reshape(specf.shape)

    def put(row, lanes, value):
        high = value.astype(jnp.bfloat16)
        s_hi[pl.ds(row, cb), lanes] = high
        s_lo[pl.ds(row, cb), lanes] = (value - high.astype(jnp.float32)).astype(jnp.bfloat16)

    for parity in range(2):
        re = pl.ds(parity * half_lanes, half_lanes)
        im = pl.ds(n + parity * half_lanes, half_lanes)
        f0r, f0i = specf[0, :, re], specf[0, :, im]
        f1r, f1i = specf[1, :, re], specf[1, :, im]
        h0r = h0i = h1r = h1i = jnp.zeros((cb, half_lanes), jnp.float32)
        for b in range(n_dp):
            g0r, g0i = spec[0, b, 0, :, re], spec[0, b, 0, :, im]
            g1r, g1i = spec[1, b, 0, :, re], spec[1, b, 0, :, im]
            x0r, x0i = spec[0, b, 1, :, re], spec[0, b, 1, :, im]
            x1r, x1i = spec[1, b, 1, :, re], spec[1, b, 1, :, im]
            if parity == 0:
                qr, qi = g0r + g1i, g0i - g1r
            else:
                qr, qi = g0r - g1i, g0i + g1r
            ar, ai = corr(x0r, x0i, qr, qi)
            br, bi = corr(x1r, x1i, g1r, g1i)
            cr, ci = corr(x0r, x0i, g1r, g1i)
            h0r, h0i = h0r + (ar + br), h0i + (ai + bi)
            h1r, h1i = h1r + cr, h1i + ci
            ar, ai = corr(f0r, f0i, qr, qi)
            br, bi = corr(f1r, f1i, g1r, g1i)
            cr, ci = corr(f0r, f0i, g1r, g1i)
            row = n_ctx * cb + b * cb
            put(row, re, ar + br)
            put(row, im, ai + bi)
            put(row + n_dp * cb, re, cr)
            put(row + n_dp * cb, im, ci)
        put(0, re, h0r)
        put(0, im, h0i)
        put(cb, re, h1r)
        put(cb, im, h1i)

    def inverse(start, size):
        high, low = s_hi[pl.ds(start, size), :], s_lo[pl.ds(start, size), :]
        total = dot_nt(high, wh[...]) + (dot_nt(low, wh[...]) + dot_nt(high, wl[...]))
        return total * (1.0 / n)

    h_out[...] = inverse(0, n_ctx * cb).reshape(h_out.shape)
    for o in remote:
        pc, pd = ahead(*o)
        peer = pc * n_dp + pd
        c = pltpu.make_async_remote_copy(
            src_ref=h_out.at[pc], dst_ref=h_in.at[me],
            send_sem=send_h.at[peer], recv_sem=recv_h.at[me],
            device_id={"context": pc, "dp": pd}, device_id_type=MESH,
        )
        c.start()
        sent.append(c)
    dx_out[...] = inverse(n_ctx * cb, group * cb).astype(jnp.bfloat16).reshape(dx_out.shape)
    for o in remote:
        pc, pd = ahead(*o)
        peer = pc * n_dp + pd
        c = pltpu.make_async_remote_copy(
            src_ref=dx_out.at[pc, pd], dst_ref=dx_in.at[me],
            send_sem=send_dx.at[peer], recv_sem=recv_dx.at[me],
            device_id={"context": pc, "dp": pd}, device_id_type=MESH,
        )
        c.start()
        sent.append(c)
    h_in[me] = h_out[ctx]
    dx_in[me] = dx_out[ctx, dp]
    for o in remote:
        sc, sd = behind(*o)
        source = sc * n_dp + sd
        pltpu.make_async_remote_copy(
            src_ref=h_out.at[0], dst_ref=h_in.at[source],
            send_sem=send_h.at[me], recv_sem=recv_h.at[source],
            device_id={"context": sc, "dp": sd}, device_id_type=MESH,
        ).wait_recv()
    h_ref[...] = h_in[...].reshape(width, n).T
    for o in remote:
        sc, sd = behind(*o)
        source = sc * n_dp + sd
        pltpu.make_async_remote_copy(
            src_ref=dx_out.at[0, 0], dst_ref=dx_in.at[source],
            send_sem=send_dx.at[me], recv_sem=recv_dx.at[source],
            device_id={"context": sc, "dp": sd}, device_id_type=MESH,
        ).wait_recv()
    dx_ref[...] = dx_in[...].reshape(width, n).T
    for c in sent:
        c.wait_send()


def fused_body(n_ctx, n_dp, grad_out, inputs, filt):
    n, width = filt.shape
    group = n_ctx * n_dp
    cb = width // group
    high, low = half_step_table(n)
    bf16, f32 = jnp.bfloat16, jnp.float32
    sems = pltpu.SemaphoreType.DMA
    any_spec = pl.BlockSpec(memory_space=pl.ANY)
    vmem_spec = pl.BlockSpec(memory_space=pltpu.VMEM)
    dx, h = pl.pallas_call(
        functools.partial(kernel, n_ctx, n_dp),
        out_shape=(
            jax.ShapeDtypeStruct((n, width), bf16),
            jax.ShapeDtypeStruct((n, width), f32),
        ),
        in_specs=[any_spec] * 5,
        out_specs=(vmem_spec, vmem_spec),
        scratch_shapes=[
            pltpu.VMEM((n, width), bf16),
            pltpu.VMEM((n, width), bf16),
            pltpu.VMEM((n, width), bf16),
            pltpu.VMEM((n, 2 * n), bf16),
            pltpu.VMEM((n, 2 * n), bf16),
            pltpu.VMEM((group, 2, cb, n), bf16),
            pltpu.VMEM((group, cb, n), bf16),
            pltpu.VMEM((n_ctx, n_dp, 2, cb, n), bf16),
            pltpu.VMEM((n_ctx, cb, n), bf16),
            pltpu.VMEM((n_ctx, n_dp, 2, cb, 2 * n), f32),
            pltpu.VMEM((n_ctx, cb, 2 * n), f32),
            pltpu.VMEM((n_ctx * cb + group * cb, 2 * n), bf16),
            pltpu.VMEM((n_ctx * cb + group * cb, 2 * n), bf16),
            pltpu.VMEM((n_ctx, cb, n), f32),
            pltpu.VMEM((n_ctx, n_dp, cb, n), bf16),
            pltpu.VMEM((group, cb, n), f32),
            pltpu.VMEM((group, cb, n), bf16),
            sems((5,)),
            sems((group,)), sems((group,)),
            sems((n_ctx,)), sems((n_ctx,)),
            sems((group,)), sems((group,)),
            sems((group,)), sems((group,)),
        ],
        compiler_params=pltpu.CompilerParams(
            collective_id=0, has_side_effects=True, vmem_limit_bytes=40 * 1024 * 1024
        ),
    )(
        grad_out.reshape(n, width), inputs.reshape(n, width), filt,
        jnp.asarray(high), jnp.asarray(low),
    )
    return dx.reshape(grad_out.shape), h


full_turn = 2.0 * math.pi


def rotation(left_idx, right_idx, modulus):
    angle = (left_idx * right_idx % modulus).astype(jnp.float32) * (full_turn / modulus)
    return (jnp.cos(angle), jnp.sin(angle))


def contract(form, table, values):
    return jnp.einsum(
        form, table, values, precision=lax.Precision.HIGHEST, preferred_element_type=jnp.float32
    )


def first_section(part, cos_first, sin_first, cos_twist, sin_twist, members, piece_rows):
    values = part.astype(jnp.float32)
    values = values.reshape(values.shape[0], members, piece_rows, values.shape[2])
    real_part = contract("fn,knbc->kfbc", cos_first, values)
    imag_part = -contract("fn,knbc->kfbc", sin_first, values)
    cos_wide = cos_twist[None, :, :, None]
    sin_wide = sin_twist[None, :, :, None]
    return jnp.stack(
        [real_part * cos_wide + imag_part * sin_wide, imag_part * cos_wide - real_part * sin_wide]
    )


def second_section(mixed, cos_second, sin_second):
    real_in = mixed[0]
    imag_in = mixed[1]
    real_out = contract("fn,kgnc->kgfc", cos_second, real_in) + contract(
        "fn,kgnc->kgfc", sin_second, imag_in
    )
    imag_out = contract("fn,kgnc->kgfc", cos_second, imag_in) - contract(
        "fn,kgnc->kgfc", sin_second, real_in
    )
    return (real_out, imag_out)


def body(grad_out, inputs, filt):
    members = lax.axis_size("context")
    position = lax.axis_index("context")
    seq_rows = grad_out.shape[1]
    piece_rows = seq_rows // members
    spread = 2 * members
    modulus = spread * seq_rows
    freq_first = jnp.arange(spread, dtype=jnp.int32)
    dev_first = jnp.arange(members, dtype=jnp.int32)
    cos_first, sin_first = rotation(freq_first[:, None], dev_first[None, :], spread)
    local_rows = position * piece_rows + jnp.arange(piece_rows, dtype=jnp.int32)
    cos_twist, sin_twist = rotation(freq_first[:, None], local_rows[None, :], modulus)
    all_rows = jnp.arange(seq_rows, dtype=jnp.int32)
    cos_second, sin_second = rotation(all_rows[:, None], all_rows[None, :], seq_rows)
    signals = jnp.concatenate([grad_out, inputs], axis=0)
    replicas = lax.axis_size("dp")
    width = filt.shape[1] // replicas
    own_filter = lax.dynamic_slice_in_dim(filt, lax.axis_index("dp") * width, width, 1)[None]
    column_sig, column_filt = (
        lax.all_to_all(signals, "context", split_axis=1, concat_axis=1, tiled=True),
        lax.all_to_all(own_filter, "context", split_axis=1, concat_axis=1, tiled=True),
    )
    sectioned_sig = first_section(
        column_sig, cos_first, sin_first, cos_twist, sin_twist, members, piece_rows
    )
    sectioned_filt = first_section(
        column_filt, cos_first, sin_first, cos_twist, sin_twist, members, piece_rows
    )
    mixed_sig, mixed_filt = (
        lax.all_to_all(sectioned_sig, "context", split_axis=2, concat_axis=3, tiled=True),
        lax.all_to_all(sectioned_filt, "context", split_axis=2, concat_axis=3, tiled=True),
    )
    sig_re, sig_im = second_section(mixed_sig, cos_second, sin_second)
    filt_re, filt_im = second_section(mixed_filt, cos_second, sin_second)
    filt_re, filt_im = (
        lax.all_gather(filt_re, "dp", axis=3, tiled=True),
        lax.all_gather(filt_im, "dp", axis=3, tiled=True),
    )
    grad_re = sig_re[0]
    grad_im = sig_im[0]
    input_re = sig_re[1]
    input_im = sig_im[1]
    kernel_re = filt_re[0]
    kernel_im = filt_im[0]
    dx_re = grad_re * kernel_re + grad_im * kernel_im
    dx_im = grad_im * kernel_re - grad_re * kernel_im
    dh_re = grad_re * input_re + grad_im * input_im
    dh_im = grad_im * input_re - grad_re * input_im
    spec_re = jnp.stack([dx_re, dh_re])
    spec_im = jnp.stack([dx_im, dh_im])
    back_re = contract("nf,sgfc->sgnc", cos_second, spec_re) - contract(
        "nf,sgfc->sgnc", sin_second, spec_im
    )
    back_im = contract("nf,sgfc->sgnc", cos_second, spec_im) + contract(
        "nf,sgfc->sgnc", sin_second, spec_re
    )
    own_freq = 2 * position + jnp.arange(2, dtype=jnp.int32)
    cos_back, sin_back = rotation(own_freq[:, None], all_rows[None, :], modulus)
    cos_wide = cos_back[None, :, :, None]
    sin_wide = sin_back[None, :, :, None]
    turned = jnp.stack(
        [back_re * cos_wide - back_im * sin_wide, back_im * cos_wide + back_re * sin_wide]
    )
    regrouped = lax.all_to_all(turned, "context", split_axis=3, concat_axis=2, tiled=True)
    in_time = contract("fn,sfbc->snbc", cos_first, regrouped[0]) - contract(
        "fn,sfbc->snbc", sin_first, regrouped[1]
    )
    in_time = in_time * (1.0 / modulus)
    restored = lax.all_to_all(in_time, "context", split_axis=1, concat_axis=2, tiled=True)
    input_grad = restored[0].astype(jnp.bfloat16)
    filter_grad = lax.psum(restored[1, 0], "dp")
    return (input_grad, filter_grad)


def any_body(n_ctx, n_dp, grad_out, inputs, filt):
    n, width = filt.shape
    tile = 32
    fits = (
        n_ctx == 2
        and grad_out.shape[0] == 1
        and n % 256 == 0
        and width % (n_ctx * n_dp * tile) == 0
        and 16 * n * (n + width) * 4 <= 40 * 1024 * 1024
    )
    if fits:
        return fused_body(n_ctx, n_dp, grad_out, inputs, filt)
    return body(grad_out, inputs, filt)


def solution(mesh):
    return jax.shard_map(
        functools.partial(any_body, mesh.shape["context"], mesh.shape["dp"]),
        mesh=mesh,
        in_specs=(
            P("dp", "context", "tensor"),
            P("dp", "context", "tensor"),
            P("context", "tensor"),
        ),
        out_specs=(P("dp", "context", "tensor"), P("context", "tensor")),
        check_vma=False,
    )
```

```python
import functools
import math

import jax
import jax.numpy as jnp
import ml_dtypes
import numpy as np
from jax import lax
from jax.experimental import pallas as pl
from jax.experimental.pallas import tpu as pltpu
from jax.sharding import PartitionSpec as P

MESH = pl.DeviceIdType.MESH
NT = (((1,), (1,)), ((), ()))


def half_step_table(n):
    k = np.concatenate([np.arange(0, n, 2), np.arange(1, n, 2)])
    turns = (np.arange(n)[:, None] * (2 * k[None, :] + 1)) % (4 * n)
    angle = turns * (math.pi / (2 * n))
    table = np.concatenate([np.cos(angle), -np.sin(angle)], axis=1)
    high = table.astype(ml_dtypes.bfloat16)
    low = (table - high.astype(np.float64)).astype(ml_dtypes.bfloat16)
    return high, low


def dot(a, b):
    return jnp.dot(a, b, preferred_element_type=jnp.float32)


def dot_nt(a, b):
    return lax.dot_general(a, b, NT, preferred_element_type=jnp.float32)


def corr(fr, fi, gr, gi):
    return fr * gr + fi * gi, fr * gi - fi * gr


def kernel(
    n_ctx, n_dp,
    g_hbm, x_hbm, f_hbm, wh_hbm, wl_hbm,
    dx_ref, h_ref,
    g_in, x_in, f_in, wh, wl,
    out1, outf, in1, inf, spec, specf, s_hi, s_lo, h_out, dx_out, h_in, dx_in,
    load_sem, send1, recv1, sendf, recvf, send_h, recv_h, send_f, send_dx, recv_dx,
):
    n, width = g_hbm.shape
    group = n_ctx * n_dp
    cb = width // group
    half_lanes = n // 2
    ctx = lax.axis_index("context")
    dp = lax.axis_index("dp")
    me = ctx * n_dp + dp

    barrier = pltpu.get_barrier_semaphore()
    offsets = [(dc, dd) for dc in range(n_ctx - 1, -1, -1) for dd in range(n_dp - 1, -1, -1)]
    remote = [o for o in offsets if o != (0, 0)]

    def ahead(dc, dd):
        return lax.rem(ctx + dc, n_ctx), lax.rem(dp + dd, n_dp)

    def behind(dc, dd):
        return lax.rem(ctx + n_ctx - dc, n_ctx), lax.rem(dp + n_dp - dd, n_dp)

    for o in remote:
        pc, pd = ahead(*o)
        pl.semaphore_signal(barrier, inc=1, device_id={"context": pc, "dp": pd}, device_id_type=MESH)
    loads = [
        pltpu.make_async_copy(src, dst, load_sem.at[i])
        for i, (src, dst) in enumerate(
            [(g_hbm, g_in), (x_hbm, x_in), (f_hbm, f_in), (wh_hbm, wh), (wl_hbm, wl)]
        )
    ]
    for c in loads:
        c.start()

    sib = dp + 1 - 2 * lax.rem(dp, 2)
    sent = []

    def push(src, dst, send, recv, pc, pd):
        c = pltpu.make_async_remote_copy(
            src_ref=src, dst_ref=dst, send_sem=send, recv_sem=recv,
            device_id={"context": pc, "dp": pd}, device_id_type=MESH,
        )
        c.start()
        sent.append(c)

    def arrived(src, dst, send, recv, pc, pd):
        pltpu.make_async_remote_copy(
            src_ref=src, dst_ref=dst, send_sem=send, recv_sem=recv,
            device_id={"context": pc, "dp": pd}, device_id_type=MESH,
        ).wait_recv()

    part = n_dp * cb

    def turn(src, c):
        lanes = pl.ds(pl.multiple_of(c * part, part), part)
        return src[:, lanes].T.reshape(n_dp, cb, n)

    for i, src in enumerate((g_in, x_in)):
        loads[i].wait()
    for dc in range(n_ctx - 1, -1, -1):
        pc, _ = ahead(dc, 0)
        blocks = pl.ds(pc * n_dp, n_dp)
        out1[blocks, 0] = turn(g_in, pc)
        out1[blocks, 1] = turn(x_in, pc)
        if dc == n_ctx - 1:
            pl.semaphore_wait(barrier, group - 1)
        for dd in range(n_dp - 1, -1, -1):
            if (dc, dd) != (0, 0):
                _, pd = ahead(dc, dd)
                peer = pc * n_dp + pd
                push(out1.at[peer], in1.at[ctx, dp], send1.at[peer], recv1.at[me], pc, pd)
    loads[2].wait()
    outf[...] = f_in[...].T.reshape(group, cb, n)
    for dc in range(1, n_ctx):
        pc, _ = ahead(dc, 0)
        push(outf.at[pc * n_dp + dp], inf.at[ctx], sendf.at[dc], recvf.at[ctx], pc, dp)
    in1[ctx, dp] = out1[me]
    inf[ctx] = outf[me]
    loads[3].wait()
    loads[4].wait()

    for dc in range(n_ctx):
        sc, _ = behind(dc, 0)
        for dd in range(n_dp):
            if (dc, dd) != (0, 0):
                _, sd = behind(dc, dd)
                arrived(out1.at[me], in1.at[sc, sd], send1.at[me], recv1.at[sc * n_dp + sd], sc, sd)
        rows = in1[sc].reshape(n_dp * 2 * cb, n)
        spec[sc] = (dot(rows, wh[...]) + dot(rows, wl[...])).reshape(n_dp, 2, cb, 2 * n)

    def put(row, lanes, value):
        high = value.astype(jnp.bfloat16)
        s_hi[pl.ds(row, cb), lanes] = high
        s_lo[pl.ds(row, cb), lanes] = (value - high.astype(jnp.float32)).astype(jnp.bfloat16)

    def shifted(parity, b, re, im):
        g0r, g0i = spec[0, b, 0, :, re], spec[0, b, 0, :, im]
        g1r, g1i = spec[1, b, 0, :, re], spec[1, b, 0, :, im]
        if parity == 0:
            return g0r + g1i, g0i - g1r, g1r, g1i
        return g0r - g1i, g0i + g1r, g1r, g1i

    def lanes_of(parity):
        return pl.ds(parity * half_lanes, half_lanes), pl.ds(n + parity * half_lanes, half_lanes)

    def inverse(start, size):
        rows = pl.ds(start, size)
        high, low = s_hi[rows, :], s_lo[rows, :]
        total = dot_nt(high, wh[...]) + (dot_nt(low, wh[...]) + dot_nt(high, wl[...]))
        return total * (1.0 / n)

    for parity in range(2):
        re, im = lanes_of(parity)
        h0r = h0i = h1r = h1i = jnp.zeros((cb, half_lanes), jnp.float32)
        for b in range(n_dp):
            qr, qi, g1r, g1i = shifted(parity, b, re, im)
            x0r, x0i = spec[0, b, 1, :, re], spec[0, b, 1, :, im]
            x1r, x1i = spec[1, b, 1, :, re], spec[1, b, 1, :, im]
            ar, ai = corr(x0r, x0i, qr, qi)
            br, bi = corr(x1r, x1i, g1r, g1i)
            cr, ci = corr(x0r, x0i, g1r, g1i)
            h0r, h0i = h0r + (ar + br), h0i + (ai + bi)
            h1r, h1i = h1r + cr, h1i + ci
        put(0, re, h0r)
        put(0, im, h0i)
        put(cb, re, h1r)
        put(cb, im, h1i)
    h_out[...] = inverse(0, n_ctx * cb).reshape(h_out.shape)
    for dc, dd in remote:
        if dd % 2 == 0:
            pc, pd = ahead(dc, dd)
            push(h_out.at[pc], h_in.at[me], send_h.at[pc * n_dp + pd], recv_h.at[me], pc, pd)
    push(h_out.at[ctx], h_in.at[me], send_h.at[ctx * n_dp + sib], recv_h.at[me], ctx, sib)
    h_in[me] = h_out[ctx]

    for dc in range(1, n_ctx):
        sc, _ = behind(dc, 0)
        arrived(outf.at[me], inf.at[sc], sendf.at[0], recvf.at[sc], sc, dp)
    rows_f = inf[...].reshape(n_ctx * cb, n)
    specf[...] = (dot(rows_f, wh[...]) + dot(rows_f, wl[...])).reshape(specf.shape)
    first = n_ctx * cb
    for parity in range(2):
        re, im = lanes_of(parity)
        f0r, f0i = specf[0, :, re], specf[0, :, im]
        f1r, f1i = specf[1, :, re], specf[1, :, im]
        for b in range(n_dp):
            qr, qi, g1r, g1i = shifted(parity, b, re, im)
            ar, ai = corr(f0r, f0i, qr, qi)
            br, bi = corr(f1r, f1i, g1r, g1i)
            cr, ci = corr(f0r, f0i, g1r, g1i)
            row = first + b * cb
            put(row, re, ar + br)
            put(row, im, ai + bi)
            put(row + part, re, cr)
            put(row + part, im, ci)
    for dc in range(n_ctx - 1, -1, -1):
        pc, _ = ahead(dc, 0)
        start = pl.multiple_of(first + pc * part, cb)
        dx_out[pc] = inverse(start, part).astype(jnp.bfloat16).reshape(n_dp, cb, n)
        for dd in range(n_dp - 1, -1, -1):
            if (dc, dd) != (0, 0):
                _, pd = ahead(dc, dd)
                push(dx_out.at[pc, pd], dx_in.at[me], send_dx.at[pc * n_dp + pd], recv_dx.at[me], pc, pd)
    dx_in[me] = dx_out[ctx, dp]

    def h_arrived(sc, sd):
        source = sc * n_dp + sd
        arrived(h_out.at[0], h_in.at[source], send_h.at[me], recv_h.at[source], sc, sd)
        return source

    def finish(sc, src, dst):
        lanes = pl.ds(pl.multiple_of(sc * part, part), part)
        dst[:, lanes] = src[pl.ds(sc * n_dp, n_dp)].reshape(part, n).T

    for dc in range(n_ctx):
        for dd in range(0, n_dp, 2):
            if (dc, dd) != (0, 0):
                source = h_arrived(*behind(dc, dd))
                push(h_in.at[source], h_in.at[source], send_f.at[source], recv_h.at[source], ctx, sib)
    for dc in range(n_ctx):
        for dd in range(1, n_dp, 2):
            h_arrived(*behind(dc, dd))
        finish(behind(dc, 0)[0], h_in, h_ref)
    for dc in range(n_ctx):
        sc, _ = behind(dc, 0)
        for dd in range(n_dp):
            if (dc, dd) != (0, 0):
                _, sd = behind(dc, dd)
                source = sc * n_dp + sd
                arrived(dx_out.at[0, 0], dx_in.at[source], send_dx.at[me], recv_dx.at[source], sc, sd)
        finish(sc, dx_in, dx_ref)
    for c in sent:
        c.wait_send()


def fused_body(n_ctx, n_dp, grad_out, inputs, filt):
    n, width = filt.shape
    group = n_ctx * n_dp
    cb = width // group
    high, low = half_step_table(n)
    bf16, f32 = jnp.bfloat16, jnp.float32
    sems = pltpu.SemaphoreType.DMA
    hbm_spec = pl.BlockSpec(memory_space=pltpu.HBM)
    vmem_spec = pl.BlockSpec(memory_space=pltpu.VMEM)
    dx, h = pl.pallas_call(
        functools.partial(kernel, n_ctx, n_dp),
        out_shape=(
            jax.ShapeDtypeStruct((n, width), bf16),
            jax.ShapeDtypeStruct((n, width), f32),
        ),
        in_specs=[hbm_spec] * 5,
        out_specs=(vmem_spec, vmem_spec),
        scratch_shapes=[
            pltpu.VMEM((n, width), bf16),
            pltpu.VMEM((n, width), bf16),
            pltpu.VMEM((n, width), bf16),
            pltpu.VMEM((n, 2 * n), bf16),
            pltpu.VMEM((n, 2 * n), bf16),
            pltpu.VMEM((group, 2, cb, n), bf16),
            pltpu.VMEM((group, cb, n), bf16),
            pltpu.VMEM((n_ctx, n_dp, 2, cb, n), bf16),
            pltpu.VMEM((n_ctx, cb, n), bf16),
            pltpu.VMEM((n_ctx, n_dp, 2, cb, 2 * n), f32),
            pltpu.VMEM((n_ctx, cb, 2 * n), f32),
            pltpu.VMEM((n_ctx * cb + group * cb, 2 * n), bf16),
            pltpu.VMEM((n_ctx * cb + group * cb, 2 * n), bf16),
            pltpu.VMEM((n_ctx, cb, n), f32),
            pltpu.VMEM((n_ctx, n_dp, cb, n), bf16),
            pltpu.VMEM((group, cb, n), f32),
            pltpu.VMEM((group, cb, n), bf16),
            sems((5,)),
            sems((group,)), sems((group,)),
            sems((n_ctx,)), sems((n_ctx,)),
            sems((group,)), sems((group,)), sems((group,)),
            sems((group,)), sems((group,)),
        ],
        compiler_params=pltpu.CompilerParams(
            collective_id=0, has_side_effects=True, vmem_limit_bytes=40 * 1024 * 1024
        ),
    )(
        grad_out.reshape(n, width), inputs.reshape(n, width), filt,
        jnp.asarray(high), jnp.asarray(low),
    )
    return dx.reshape(grad_out.shape), h


full_turn = 2.0 * math.pi


def rotation(left_idx, right_idx, modulus):
    angle = (left_idx * right_idx % modulus).astype(jnp.float32) * (full_turn / modulus)
    return (jnp.cos(angle), jnp.sin(angle))


def contract(form, table, values):
    return jnp.einsum(
        form, table, values, precision=lax.Precision.HIGHEST, preferred_element_type=jnp.float32
    )


def first_section(part, cos_first, sin_first, cos_twist, sin_twist, members, piece_rows):
    values = part.astype(jnp.float32)
    values = values.reshape(values.shape[0], members, piece_rows, values.shape[2])
    real_part = contract("fn,knbc->kfbc", cos_first, values)
    imag_part = -contract("fn,knbc->kfbc", sin_first, values)
    cos_wide = cos_twist[None, :, :, None]
    sin_wide = sin_twist[None, :, :, None]
    return jnp.stack(
        [real_part * cos_wide + imag_part * sin_wide, imag_part * cos_wide - real_part * sin_wide]
    )


def second_section(mixed, cos_second, sin_second):
    real_in = mixed[0]
    imag_in = mixed[1]
    real_out = contract("fn,kgnc->kgfc", cos_second, real_in) + contract(
        "fn,kgnc->kgfc", sin_second, imag_in
    )
    imag_out = contract("fn,kgnc->kgfc", cos_second, imag_in) - contract(
        "fn,kgnc->kgfc", sin_second, real_in
    )
    return (real_out, imag_out)


def body(grad_out, inputs, filt):
    members = lax.axis_size("context")
    position = lax.axis_index("context")
    seq_rows = grad_out.shape[1]
    piece_rows = seq_rows // members
    spread = 2 * members
    modulus = spread * seq_rows
    freq_first = jnp.arange(spread, dtype=jnp.int32)
    dev_first = jnp.arange(members, dtype=jnp.int32)
    cos_first, sin_first = rotation(freq_first[:, None], dev_first[None, :], spread)
    local_rows = position * piece_rows + jnp.arange(piece_rows, dtype=jnp.int32)
    cos_twist, sin_twist = rotation(freq_first[:, None], local_rows[None, :], modulus)
    all_rows = jnp.arange(seq_rows, dtype=jnp.int32)
    cos_second, sin_second = rotation(all_rows[:, None], all_rows[None, :], seq_rows)
    signals = jnp.concatenate([grad_out, inputs], axis=0)
    replicas = lax.axis_size("dp")
    width = filt.shape[1] // replicas
    own_filter = lax.dynamic_slice_in_dim(filt, lax.axis_index("dp") * width, width, 1)[None]
    column_sig, column_filt = (
        lax.all_to_all(signals, "context", split_axis=1, concat_axis=1, tiled=True),
        lax.all_to_all(own_filter, "context", split_axis=1, concat_axis=1, tiled=True),
    )
    sectioned_sig = first_section(
        column_sig, cos_first, sin_first, cos_twist, sin_twist, members, piece_rows
    )
    sectioned_filt = first_section(
        column_filt, cos_first, sin_first, cos_twist, sin_twist, members, piece_rows
    )
    mixed_sig, mixed_filt = (
        lax.all_to_all(sectioned_sig, "context", split_axis=2, concat_axis=3, tiled=True),
        lax.all_to_all(sectioned_filt, "context", split_axis=2, concat_axis=3, tiled=True),
    )
    sig_re, sig_im = second_section(mixed_sig, cos_second, sin_second)
    filt_re, filt_im = second_section(mixed_filt, cos_second, sin_second)
    filt_re, filt_im = (
        lax.all_gather(filt_re, "dp", axis=3, tiled=True),
        lax.all_gather(filt_im, "dp", axis=3, tiled=True),
    )
    grad_re = sig_re[0]
    grad_im = sig_im[0]
    input_re = sig_re[1]
    input_im = sig_im[1]
    kernel_re = filt_re[0]
    kernel_im = filt_im[0]
    dx_re = grad_re * kernel_re + grad_im * kernel_im
    dx_im = grad_im * kernel_re - grad_re * kernel_im
    dh_re = grad_re * input_re + grad_im * input_im
    dh_im = grad_im * input_re - grad_re * input_im
    spec_re = jnp.stack([dx_re, dh_re])
    spec_im = jnp.stack([dx_im, dh_im])
    back_re = contract("nf,sgfc->sgnc", cos_second, spec_re) - contract(
        "nf,sgfc->sgnc", sin_second, spec_im
    )
    back_im = contract("nf,sgfc->sgnc", cos_second, spec_im) + contract(
        "nf,sgfc->sgnc", sin_second, spec_re
    )
    own_freq = 2 * position + jnp.arange(2, dtype=jnp.int32)
    cos_back, sin_back = rotation(own_freq[:, None], all_rows[None, :], modulus)
    cos_wide = cos_back[None, :, :, None]
    sin_wide = sin_back[None, :, :, None]
    turned = jnp.stack(
        [back_re * cos_wide - back_im * sin_wide, back_im * cos_wide + back_re * sin_wide]
    )
    regrouped = lax.all_to_all(turned, "context", split_axis=3, concat_axis=2, tiled=True)
    in_time = contract("fn,sfbc->snbc", cos_first, regrouped[0]) - contract(
        "fn,sfbc->snbc", sin_first, regrouped[1]
    )
    in_time = in_time * (1.0 / modulus)
    restored = lax.all_to_all(in_time, "context", split_axis=1, concat_axis=2, tiled=True)
    input_grad = restored[0].astype(jnp.bfloat16)
    filter_grad = lax.psum(restored[1, 0], "dp")
    return (input_grad, filter_grad)


def any_body(n_ctx, n_dp, grad_out, inputs, filt):
    n, width = filt.shape
    tile = 32
    fits = (
        n_ctx == 2
        and grad_out.shape[0] == 1
        and n_dp % 2 == 0
        and n % 256 == 0
        and width % (n_ctx * n_dp * tile) == 0
        and width % (n_ctx * 128) == 0
        and 16 * n * (n + width) * 4 <= 40 * 1024 * 1024
    )
    if fits:
        return fused_body(n_ctx, n_dp, grad_out, inputs, filt)
    return body(grad_out, inputs, filt)


def solution(mesh):
    return jax.shard_map(
        functools.partial(any_body, mesh.shape["context"], mesh.shape["dp"]),
        mesh=mesh,
        in_specs=(
            P("dp", "context", "tensor"),
            P("dp", "context", "tensor"),
            P("context", "tensor"),
        ),
        out_specs=(P("dp", "context", "tensor"), P("context", "tensor")),
        check_vma=False,
    )
```

```python
import functools
import math

import jax
import jax.numpy as jnp
import ml_dtypes
import numpy as np
from jax import lax
from jax.experimental import pallas as pl
from jax.experimental.pallas import tpu as pltpu
from jax.sharding import PartitionSpec as P

MESH = pl.DeviceIdType.MESH
NT = (((1,), (1,)), ((), ()))


def half_step_table(n):
    k = np.concatenate([np.arange(0, n, 2), np.arange(1, n, 2)])
    turns = (np.arange(n)[:, None] * (2 * k[None, :] + 1)) % (4 * n)
    angle = turns * (math.pi / (2 * n))
    table = np.concatenate([np.cos(angle), -np.sin(angle)], axis=1)
    high = table.astype(ml_dtypes.bfloat16)
    low = (table - high.astype(np.float64)).astype(ml_dtypes.bfloat16)
    return high, low


def dot(a, b):
    return jnp.dot(a, b, preferred_element_type=jnp.float32)


def dot_nt(a, b):
    return lax.dot_general(a, b, NT, preferred_element_type=jnp.float32)


def corr(fr, fi, gr, gi):
    return fr * gr + fi * gi, fr * gi - fi * gr


def kernel(
    n_ctx, n_dp,
    g_hbm, x_hbm, f_hbm, wh_hbm, wl_hbm,
    dx_ref, h_ref,
    g_in, x_in, f_in, wh, wl,
    out1, outf, in1, inf, spec, specf, s_hi, s_lo, h_out, dx_out, h_in, dx_in,
    load_sem, send1, recv1, sendf, recvf, send_h, recv_h, send_f, send_dx, recv_dx,
):
    n, width = g_hbm.shape
    group = n_ctx * n_dp
    cb = width // group
    half_lanes = n // 2
    ctx = lax.axis_index("context")
    dp = lax.axis_index("dp")
    me = ctx * n_dp + dp

    barrier = pltpu.get_barrier_semaphore()
    offsets = [(dc, dd) for dc in range(n_ctx - 1, -1, -1) for dd in range(n_dp - 1, -1, -1)]
    remote = [o for o in offsets if o != (0, 0)]

    def ahead(dc, dd):
        return lax.rem(ctx + dc, n_ctx), lax.rem(dp + dd, n_dp)

    def behind(dc, dd):
        return lax.rem(ctx + n_ctx - dc, n_ctx), lax.rem(dp + n_dp - dd, n_dp)

    for o in remote:
        pc, pd = ahead(*o)
        pl.semaphore_signal(barrier, inc=1, device_id={"context": pc, "dp": pd}, device_id_type=MESH)
    loads = [
        pltpu.make_async_copy(src, dst, load_sem.at[i])
        for i, (src, dst) in enumerate(
            [(g_hbm, g_in), (x_hbm, x_in), (f_hbm, f_in), (wh_hbm, wh), (wl_hbm, wl)]
        )
    ]
    for c in loads:
        c.start()

    sib = dp + 1 - 2 * lax.rem(dp, 2)
    sent = []

    def push(src, dst, send, recv, pc, pd):
        c = pltpu.make_async_remote_copy(
            src_ref=src, dst_ref=dst, send_sem=send, recv_sem=recv,
            device_id={"context": pc, "dp": pd}, device_id_type=MESH,
        )
        c.start()
        sent.append(c)

    def arrived(src, dst, send, recv, pc, pd):
        pltpu.make_async_remote_copy(
            src_ref=src, dst_ref=dst, send_sem=send, recv_sem=recv,
            device_id={"context": pc, "dp": pd}, device_id_type=MESH,
        ).wait_recv()

    part = n_dp * cb

    def turn(src, c):
        lanes = pl.ds(pl.multiple_of(c * part, part), part)
        return src[:, lanes].T.reshape(n_dp, cb, n)

    for i, src in enumerate((g_in, x_in)):
        loads[i].wait()
    for dc in range(n_ctx - 1, -1, -1):
        pc, _ = ahead(dc, 0)
        blocks = pl.ds(pc * n_dp, n_dp)
        out1[blocks, 0] = turn(g_in, pc)
        out1[blocks, 1] = turn(x_in, pc)
        if dc == n_ctx - 1:
            pl.semaphore_wait(barrier, group - 1)
        for dd in range(n_dp - 1, -1, -1):
            if (dc, dd) != (0, 0):
                _, pd = ahead(dc, dd)
                peer = pc * n_dp + pd
                push(out1.at[peer], in1.at[ctx, dp], send1.at[peer], recv1.at[me], pc, pd)
    loads[2].wait()
    outf[...] = f_in[...].T.reshape(group, cb, n)
    for dc in range(1, n_ctx):
        pc, _ = ahead(dc, 0)
        push(outf.at[pc * n_dp + dp], inf.at[ctx], sendf.at[dc], recvf.at[ctx], pc, dp)
    in1[ctx, dp] = out1[me]
    inf[ctx] = outf[me]
    loads[3].wait()
    loads[4].wait()

    for dc in range(n_ctx):
        sc, _ = behind(dc, 0)
        for dd in range(n_dp):
            if (dc, dd) != (0, 0):
                _, sd = behind(dc, dd)
                arrived(out1.at[me], in1.at[sc, sd], send1.at[me], recv1.at[sc * n_dp + sd], sc, sd)
        rows = in1[sc].reshape(n_dp * 2 * cb, n)
        spec[sc] = (dot(rows, wh[...]) + dot(rows, wl[...])).reshape(n_dp, 2, cb, 2 * n)

    def put(row, lanes, value):
        high = value.astype(jnp.bfloat16)
        s_hi[pl.ds(row, cb), lanes] = high
        s_lo[pl.ds(row, cb), lanes] = (value - high.astype(jnp.float32)).astype(jnp.bfloat16)

    def shifted(parity, b, re, im):
        g0r, g0i = spec[0, b, 0, :, re], spec[0, b, 0, :, im]
        g1r, g1i = spec[1, b, 0, :, re], spec[1, b, 0, :, im]
        if parity == 0:
            return g0r + g1i, g0i - g1r, g1r, g1i
        return g0r - g1i, g0i + g1r, g1r, g1i

    def lanes_of(parity):
        return pl.ds(parity * half_lanes, half_lanes), pl.ds(n + parity * half_lanes, half_lanes)

    def inverse(start, size):
        rows = pl.ds(start, size)
        high, low = s_hi[rows, :], s_lo[rows, :]
        total = dot_nt(high, wh[...]) + (dot_nt(low, wh[...]) + dot_nt(high, wl[...]))
        return total * (1.0 / n)

    for parity in range(2):
        re, im = lanes_of(parity)
        h0r = h0i = h1r = h1i = jnp.zeros((cb, half_lanes), jnp.float32)
        for b in range(n_dp):
            qr, qi, g1r, g1i = shifted(parity, b, re, im)
            x0r, x0i = spec[0, b, 1, :, re], spec[0, b, 1, :, im]
            x1r, x1i = spec[1, b, 1, :, re], spec[1, b, 1, :, im]
            ar, ai = corr(x0r, x0i, qr, qi)
            br, bi = corr(x1r, x1i, g1r, g1i)
            cr, ci = corr(x0r, x0i, g1r, g1i)
            h0r, h0i = h0r + (ar + br), h0i + (ai + bi)
            h1r, h1i = h1r + cr, h1i + ci
        put(0, re, h0r)
        put(0, im, h0i)
        put(cb, re, h1r)
        put(cb, im, h1i)
    h_out[...] = inverse(0, n_ctx * cb).reshape(h_out.shape)
    for dc, dd in remote:
        if dd % 2 == 0:
            pc, pd = ahead(dc, dd)
            push(h_out.at[pc], h_in.at[me], send_h.at[pc * n_dp + pd], recv_h.at[me], pc, pd)
    push(h_out.at[ctx], h_in.at[me], send_h.at[ctx * n_dp + sib], recv_h.at[me], ctx, sib)
    h_in[me] = h_out[ctx]

    for dc in range(1, n_ctx):
        sc, _ = behind(dc, 0)
        arrived(outf.at[me], inf.at[sc], sendf.at[0], recvf.at[sc], sc, dp)
    rows_f = inf[...].reshape(n_ctx * cb, n)
    specf[...] = (dot(rows_f, wh[...]) + dot(rows_f, wl[...])).reshape(specf.shape)
    first = n_ctx * cb
    for parity in range(2):
        re, im = lanes_of(parity)
        f0r, f0i = specf[0, :, re], specf[0, :, im]
        f1r, f1i = specf[1, :, re], specf[1, :, im]
        for b in range(n_dp):
            qr, qi, g1r, g1i = shifted(parity, b, re, im)
            ar, ai = corr(f0r, f0i, qr, qi)
            br, bi = corr(f1r, f1i, g1r, g1i)
            cr, ci = corr(f0r, f0i, g1r, g1i)
            row = first + b * cb
            put(row, re, ar + br)
            put(row, im, ai + bi)
            put(row + part, re, cr)
            put(row + part, im, ci)
    for dc in range(n_ctx - 1, -1, -1):
        pc, _ = ahead(dc, 0)
        start = pl.multiple_of(first + pc * part, cb)
        dx_out[pc] = inverse(start, part).astype(jnp.bfloat16).reshape(n_dp, cb, n)
        for dd in range(n_dp - 1, -1, -1):
            if (dc, dd) != (0, 0):
                _, pd = ahead(dc, dd)
                push(dx_out.at[pc, pd], dx_in.at[me], send_dx.at[pc * n_dp + pd], recv_dx.at[me], pc, pd)
    dx_in[me] = dx_out[ctx, dp]

    def h_arrived(sc, sd):
        source = sc * n_dp + sd
        arrived(h_out.at[0], h_in.at[source], send_h.at[me], recv_h.at[source], sc, sd)
        return source

    def finish(sc, src, dst):
        lanes = pl.ds(pl.multiple_of(sc * part, part), part)
        dst[:, lanes] = src[pl.ds(sc * n_dp, n_dp)].reshape(part, n).T

    for dc in range(n_ctx):
        for dd in range(0, n_dp, 2):
            if (dc, dd) != (0, 0):
                source = h_arrived(*behind(dc, dd))
                push(h_in.at[source], h_in.at[source], send_f.at[source], recv_h.at[source], ctx, sib)
    for dc in range(n_ctx):
        for dd in range(1, n_dp, 2):
            h_arrived(*behind(dc, dd))
        finish(behind(dc, 0)[0], h_in, h_ref)
    for dc in range(n_ctx):
        sc, _ = behind(dc, 0)
        for dd in range(n_dp):
            if (dc, dd) != (0, 0):
                _, sd = behind(dc, dd)
                source = sc * n_dp + sd
                arrived(dx_out.at[0, 0], dx_in.at[source], send_dx.at[me], recv_dx.at[source], sc, sd)
        finish(sc, dx_in, dx_ref)
    for c in sent:
        c.wait_send()


def fused_body(n_ctx, n_dp, grad_out, inputs, filt):
    n, width = filt.shape
    group = n_ctx * n_dp
    cb = width // group
    high, low = half_step_table(n)
    bf16, f32 = jnp.bfloat16, jnp.float32
    sems = pltpu.SemaphoreType.DMA
    hbm_spec = pl.BlockSpec(memory_space=pltpu.HBM)
    vmem_spec = pl.BlockSpec(memory_space=pltpu.VMEM)
    dx, h = pl.pallas_call(
        functools.partial(kernel, n_ctx, n_dp),
        out_shape=(
            jax.ShapeDtypeStruct((n, width), bf16),
            jax.ShapeDtypeStruct((n, width), f32),
        ),
        in_specs=[hbm_spec] * 5,
        out_specs=(vmem_spec, vmem_spec),
        scratch_shapes=[
            pltpu.VMEM((n, width), bf16),
            pltpu.VMEM((n, width), bf16),
            pltpu.VMEM((n, width), bf16),
            pltpu.VMEM((n, 2 * n), bf16),
            pltpu.VMEM((n, 2 * n), bf16),
            pltpu.VMEM((group, 2, cb, n), bf16),
            pltpu.VMEM((group, cb, n), bf16),
            pltpu.VMEM((n_ctx, n_dp, 2, cb, n), bf16),
            pltpu.VMEM((n_ctx, cb, n), bf16),
            pltpu.VMEM((n_ctx, n_dp, 2, cb, 2 * n), f32),
            pltpu.VMEM((n_ctx, cb, 2 * n), f32),
            pltpu.VMEM((n_ctx * cb + group * cb, 2 * n), bf16),
            pltpu.VMEM((n_ctx * cb + group * cb, 2 * n), bf16),
            pltpu.VMEM((n_ctx, cb, n), f32),
            pltpu.VMEM((n_ctx, n_dp, cb, n), bf16),
            pltpu.VMEM((group, cb, n), f32),
            pltpu.VMEM((group, cb, n), bf16),
            sems((5,)),
            sems((group,)), sems((group,)),
            sems((n_ctx,)), sems((n_ctx,)),
            sems((group,)), sems((group,)), sems((group,)),
            sems((group,)), sems((group,)),
        ],
        compiler_params=pltpu.CompilerParams(
            collective_id=0, has_side_effects=True, vmem_limit_bytes=40 * 1024 * 1024
        ),
    )(*(
        pltpu.with_memory_space_constraint(a, pltpu.HBM)
        for a in (
            grad_out.reshape(n, width), inputs.reshape(n, width), filt,
            jnp.asarray(high), jnp.asarray(low),
        )
    ))
    return dx.reshape(grad_out.shape), h


full_turn = 2.0 * math.pi


def rotation(left_idx, right_idx, modulus):
    angle = (left_idx * right_idx % modulus).astype(jnp.float32) * (full_turn / modulus)
    return (jnp.cos(angle), jnp.sin(angle))


def contract(form, table, values):
    return jnp.einsum(
        form, table, values, precision=lax.Precision.HIGHEST, preferred_element_type=jnp.float32
    )


def first_section(part, cos_first, sin_first, cos_twist, sin_twist, members, piece_rows):
    values = part.astype(jnp.float32)
    values = values.reshape(values.shape[0], members, piece_rows, values.shape[2])
    real_part = contract("fn,knbc->kfbc", cos_first, values)
    imag_part = -contract("fn,knbc->kfbc", sin_first, values)
    cos_wide = cos_twist[None, :, :, None]
    sin_wide = sin_twist[None, :, :, None]
    return jnp.stack(
        [real_part * cos_wide + imag_part * sin_wide, imag_part * cos_wide - real_part * sin_wide]
    )


def second_section(mixed, cos_second, sin_second):
    real_in = mixed[0]
    imag_in = mixed[1]
    real_out = contract("fn,kgnc->kgfc", cos_second, real_in) + contract(
        "fn,kgnc->kgfc", sin_second, imag_in
    )
    imag_out = contract("fn,kgnc->kgfc", cos_second, imag_in) - contract(
        "fn,kgnc->kgfc", sin_second, real_in
    )
    return (real_out, imag_out)


def body(grad_out, inputs, filt):
    members = lax.axis_size("context")
    position = lax.axis_index("context")
    seq_rows = grad_out.shape[1]
    piece_rows = seq_rows // members
    spread = 2 * members
    modulus = spread * seq_rows
    freq_first = jnp.arange(spread, dtype=jnp.int32)
    dev_first = jnp.arange(members, dtype=jnp.int32)
    cos_first, sin_first = rotation(freq_first[:, None], dev_first[None, :], spread)
    local_rows = position * piece_rows + jnp.arange(piece_rows, dtype=jnp.int32)
    cos_twist, sin_twist = rotation(freq_first[:, None], local_rows[None, :], modulus)
    all_rows = jnp.arange(seq_rows, dtype=jnp.int32)
    cos_second, sin_second = rotation(all_rows[:, None], all_rows[None, :], seq_rows)
    signals = jnp.concatenate([grad_out, inputs], axis=0)
    replicas = lax.axis_size("dp")
    width = filt.shape[1] // replicas
    own_filter = lax.dynamic_slice_in_dim(filt, lax.axis_index("dp") * width, width, 1)[None]
    column_sig, column_filt = (
        lax.all_to_all(signals, "context", split_axis=1, concat_axis=1, tiled=True),
        lax.all_to_all(own_filter, "context", split_axis=1, concat_axis=1, tiled=True),
    )
    sectioned_sig = first_section(
        column_sig, cos_first, sin_first, cos_twist, sin_twist, members, piece_rows
    )
    sectioned_filt = first_section(
        column_filt, cos_first, sin_first, cos_twist, sin_twist, members, piece_rows
    )
    mixed_sig, mixed_filt = (
        lax.all_to_all(sectioned_sig, "context", split_axis=2, concat_axis=3, tiled=True),
        lax.all_to_all(sectioned_filt, "context", split_axis=2, concat_axis=3, tiled=True),
    )
    sig_re, sig_im = second_section(mixed_sig, cos_second, sin_second)
    filt_re, filt_im = second_section(mixed_filt, cos_second, sin_second)
    filt_re, filt_im = (
        lax.all_gather(filt_re, "dp", axis=3, tiled=True),
        lax.all_gather(filt_im, "dp", axis=3, tiled=True),
    )
    grad_re = sig_re[0]
    grad_im = sig_im[0]
    input_re = sig_re[1]
    input_im = sig_im[1]
    kernel_re = filt_re[0]
    kernel_im = filt_im[0]
    dx_re = grad_re * kernel_re + grad_im * kernel_im
    dx_im = grad_im * kernel_re - grad_re * kernel_im
    dh_re = grad_re * input_re + grad_im * input_im
    dh_im = grad_im * input_re - grad_re * input_im
    spec_re = jnp.stack([dx_re, dh_re])
    spec_im = jnp.stack([dx_im, dh_im])
    back_re = contract("nf,sgfc->sgnc", cos_second, spec_re) - contract(
        "nf,sgfc->sgnc", sin_second, spec_im
    )
    back_im = contract("nf,sgfc->sgnc", cos_second, spec_im) + contract(
        "nf,sgfc->sgnc", sin_second, spec_re
    )
    own_freq = 2 * position + jnp.arange(2, dtype=jnp.int32)
    cos_back, sin_back = rotation(own_freq[:, None], all_rows[None, :], modulus)
    cos_wide = cos_back[None, :, :, None]
    sin_wide = sin_back[None, :, :, None]
    turned = jnp.stack(
        [back_re * cos_wide - back_im * sin_wide, back_im * cos_wide + back_re * sin_wide]
    )
    regrouped = lax.all_to_all(turned, "context", split_axis=3, concat_axis=2, tiled=True)
    in_time = contract("fn,sfbc->snbc", cos_first, regrouped[0]) - contract(
        "fn,sfbc->snbc", sin_first, regrouped[1]
    )
    in_time = in_time * (1.0 / modulus)
    restored = lax.all_to_all(in_time, "context", split_axis=1, concat_axis=2, tiled=True)
    input_grad = restored[0].astype(jnp.bfloat16)
    filter_grad = lax.psum(restored[1, 0], "dp")
    return (input_grad, filter_grad)


def any_body(n_ctx, n_dp, grad_out, inputs, filt):
    n, width = filt.shape
    tile = 32
    fits = (
        n_ctx == 2
        and grad_out.shape[0] == 1
        and n_dp % 2 == 0
        and n % 256 == 0
        and width % (n_ctx * n_dp * tile) == 0
        and width % (n_ctx * 128) == 0
        and 16 * n * (n + width) * 4 <= 40 * 1024 * 1024
    )
    if fits:
        return fused_body(n_ctx, n_dp, grad_out, inputs, filt)
    return body(grad_out, inputs, filt)


def solution(mesh):
    return jax.shard_map(
        functools.partial(any_body, mesh.shape["context"], mesh.shape["dp"]),
        mesh=mesh,
        in_specs=(
            P("dp", "context", "tensor"),
            P("dp", "context", "tensor"),
            P("context", "tensor"),
        ),
        out_specs=(P("dp", "context", "tensor"), P("context", "tensor")),
        check_vma=False,
    )
```

```python
import functools
import math

import jax
import jax.numpy as jnp
import ml_dtypes
import numpy as np
from jax import lax
from jax.experimental import pallas as pl
from jax.experimental.pallas import tpu as pltpu
from jax.sharding import PartitionSpec as P

MESH = pl.DeviceIdType.MESH
NT = (((1,), (1,)), ((), ()))


def half_step_table(n):
    k = np.concatenate([np.arange(0, n, 2), np.arange(1, n, 2)])
    turns = (np.arange(n)[:, None] * (2 * k[None, :] + 1)) % (4 * n)
    angle = turns * (math.pi / (2 * n))
    table = np.concatenate([np.cos(angle), -np.sin(angle)], axis=1)
    high = table.astype(ml_dtypes.bfloat16)
    low = (table - high.astype(np.float64)).astype(ml_dtypes.bfloat16)
    return high, low


def dot(a, b):
    return jnp.dot(a, b, preferred_element_type=jnp.float32)


def dot_nt(a, b):
    return lax.dot_general(a, b, NT, preferred_element_type=jnp.float32)


def corr(fr, fi, gr, gi):
    return fr * gr + fi * gi, fr * gi - fi * gr


def kernel(
    n_ctx, n_dp,
    g_hbm, x_hbm, f_hbm, wh_hbm, wl_hbm,
    dx_ref, h_ref,
    g_in, x_in, f_in, wh, wl,
    out1, outf, in1, inf, spec, specf, s_hi, s_lo, h_out, dx_out, h_in, dx_in,
    load_sem, send1, recv1, sendf, recvf, send_h, recv_h, send_f, send_dx, recv_dx,
):
    n, width = g_hbm.shape
    group = n_ctx * n_dp
    cb = width // group
    half_lanes = n // 2
    ctx = lax.axis_index("context")
    dp = lax.axis_index("dp")
    me = ctx * n_dp + dp

    barrier = pltpu.get_barrier_semaphore()
    offsets = [(dc, dd) for dc in range(n_ctx - 1, -1, -1) for dd in range(n_dp - 1, -1, -1)]
    remote = [o for o in offsets if o != (0, 0)]

    def ahead(dc, dd):
        return lax.rem(ctx + dc, n_ctx), lax.rem(dp + dd, n_dp)

    def behind(dc, dd):
        return lax.rem(ctx + n_ctx - dc, n_ctx), lax.rem(dp + n_dp - dd, n_dp)

    for o in remote:
        pc, pd = ahead(*o)
        pl.semaphore_signal(barrier, inc=1, device_id={"context": pc, "dp": pd}, device_id_type=MESH)
    loads = [
        pltpu.make_async_copy(src, dst, load_sem.at[i])
        for i, (src, dst) in enumerate(
            [(g_hbm, g_in), (x_hbm, x_in), (f_hbm, f_in), (wh_hbm, wh), (wl_hbm, wl)]
        )
    ]
    for c in loads:
        c.start()

    sib = dp + 1 - 2 * lax.rem(dp, 2)
    sent = []

    def push(src, dst, send, recv, pc, pd):
        c = pltpu.make_async_remote_copy(
            src_ref=src, dst_ref=dst, send_sem=send, recv_sem=recv,
            device_id={"context": pc, "dp": pd}, device_id_type=MESH,
        )
        c.start()
        sent.append(c)

    def arrived(src, dst, send, recv, pc, pd):
        pltpu.make_async_remote_copy(
            src_ref=src, dst_ref=dst, send_sem=send, recv_sem=recv,
            device_id={"context": pc, "dp": pd}, device_id_type=MESH,
        ).wait_recv()

    part = n_dp * cb

    def turn(src, c):
        lanes = pl.ds(pl.multiple_of(c * part, part), part)
        return src[:, lanes].T.reshape(n_dp, cb, n)

    def spread_out(sig, src, dc):
        pc, _ = ahead(dc, 0)
        out1[sig, pl.ds(pc * n_dp, n_dp)] = turn(src, pc)
        if sig == 0 and dc == n_ctx - 1:
            pl.semaphore_wait(barrier, group - 1)
        for dd in range(n_dp - 1, -1, -1):
            if (dc, dd) != (0, 0):
                _, pd = ahead(dc, dd)
                peer = pc * n_dp + pd
                push(
                    out1.at[sig, peer], in1.at[sig, ctx, dp],
                    send1.at[sig, peer], recv1.at[sig, me], pc, pd,
                )

    loads[0].wait()
    for dc in range(n_ctx - 1, 0, -1):
        spread_out(0, g_in, dc)
    loads[2].wait()
    for dc in range(n_ctx - 1, 0, -1):
        pc, _ = ahead(dc, 0)
        outf[pl.ds(pc * n_dp, n_dp)] = turn(f_in, pc)
        push(outf.at[pc * n_dp + dp], inf.at[ctx], sendf.at[dc], recvf.at[ctx], pc, dp)
    spread_out(0, g_in, 0)
    loads[1].wait()
    for dc in range(n_ctx - 1, -1, -1):
        spread_out(1, x_in, dc)
    outf[pl.ds(ctx * n_dp, n_dp)] = turn(f_in, ctx)
    in1[0, ctx, dp] = out1[0, me]
    in1[1, ctx, dp] = out1[1, me]
    inf[ctx] = outf[me]
    loads[3].wait()
    loads[4].wait()

    def collect(sig, dc):
        sc, _ = behind(dc, 0)
        for dd in range(n_dp):
            if (dc, dd) != (0, 0):
                _, sd = behind(dc, dd)
                arrived(
                    out1.at[sig, me], in1.at[sig, sc, sd],
                    send1.at[sig, me], recv1.at[sig, sc * n_dp + sd], sc, sd,
                )
        rows = in1[sig, sc].reshape(part, n)
        spec[sig, sc] = (dot(rows, wh[...]) + dot(rows, wl[...])).reshape(n_dp, cb, 2 * n)

    def put(row, lanes, value):
        high = value.astype(jnp.bfloat16)
        s_hi[pl.ds(row, cb), lanes] = high
        s_lo[pl.ds(row, cb), lanes] = (value - high.astype(jnp.float32)).astype(jnp.bfloat16)

    def shifted(parity, b, re, im):
        g0r, g0i = spec[0, 0, b, :, re], spec[0, 0, b, :, im]
        g1r, g1i = spec[0, 1, b, :, re], spec[0, 1, b, :, im]
        if parity == 0:
            return g0r + g1i, g0i - g1r, g1r, g1i
        return g0r - g1i, g0i + g1r, g1r, g1i

    def lanes_of(parity):
        return pl.ds(parity * half_lanes, half_lanes), pl.ds(n + parity * half_lanes, half_lanes)

    def inverse(start, size):
        rows = pl.ds(start, size)
        high, low = s_hi[rows, :], s_lo[rows, :]
        total = dot_nt(high, wh[...]) + (dot_nt(low, wh[...]) + dot_nt(high, wl[...]))
        return total * (1.0 / n)

    collect(0, 0)
    for dc in range(1, n_ctx):
        sc, _ = behind(dc, 0)
        arrived(outf.at[me], inf.at[sc], sendf.at[0], recvf.at[sc], sc, dp)
    rows_f = inf[...].reshape(n_ctx * cb, n)
    specf[...] = (dot(rows_f, wh[...]) + dot(rows_f, wl[...])).reshape(specf.shape)
    for dc in range(1, n_ctx):
        collect(0, dc)
    first = n_ctx * cb
    for parity in range(2):
        re, im = lanes_of(parity)
        f0r, f0i = specf[0, :, re], specf[0, :, im]
        f1r, f1i = specf[1, :, re], specf[1, :, im]
        for b in range(n_dp):
            qr, qi, g1r, g1i = shifted(parity, b, re, im)
            ar, ai = corr(f0r, f0i, qr, qi)
            br, bi = corr(f1r, f1i, g1r, g1i)
            cr, ci = corr(f0r, f0i, g1r, g1i)
            row = first + b * cb
            put(row, re, ar + br)
            put(row, im, ai + bi)
            put(row + part, re, cr)
            put(row + part, im, ci)
    for dc in range(n_ctx - 1, -1, -1):
        pc, _ = ahead(dc, 0)
        start = pl.multiple_of(first + pc * part, cb)
        dx_out[pc] = inverse(start, part).astype(jnp.bfloat16).reshape(n_dp, cb, n)
        for dd in range(n_dp - 1, -1, -1):
            if (dc, dd) != (0, 0):
                _, pd = ahead(dc, dd)
                push(dx_out.at[pc, pd], dx_in.at[me], send_dx.at[pc * n_dp + pd], recv_dx.at[me], pc, pd)
    dx_in[me] = dx_out[ctx, dp]

    for dc in range(n_ctx):
        collect(1, dc)
    for parity in range(2):
        re, im = lanes_of(parity)
        h0r = h0i = h1r = h1i = jnp.zeros((cb, half_lanes), jnp.float32)
        for b in range(n_dp):
            qr, qi, g1r, g1i = shifted(parity, b, re, im)
            x0r, x0i = spec[1, 0, b, :, re], spec[1, 0, b, :, im]
            x1r, x1i = spec[1, 1, b, :, re], spec[1, 1, b, :, im]
            ar, ai = corr(x0r, x0i, qr, qi)
            br, bi = corr(x1r, x1i, g1r, g1i)
            cr, ci = corr(x0r, x0i, g1r, g1i)
            h0r, h0i = h0r + (ar + br), h0i + (ai + bi)
            h1r, h1i = h1r + cr, h1i + ci
        put(0, re, h0r)
        put(0, im, h0i)
        put(cb, re, h1r)
        put(cb, im, h1i)
    h_out[...] = inverse(0, n_ctx * cb).reshape(h_out.shape)
    for dc, dd in remote:
        if dd % 2 == 0:
            pc, pd = ahead(dc, dd)
            push(h_out.at[pc], h_in.at[me], send_h.at[pc * n_dp + pd], recv_h.at[me], pc, pd)
    push(h_out.at[ctx], h_in.at[me], send_h.at[ctx * n_dp + sib], recv_h.at[me], ctx, sib)
    h_in[me] = h_out[ctx]

    def h_arrived(sc, sd):
        source = sc * n_dp + sd
        arrived(h_out.at[0], h_in.at[source], send_h.at[me], recv_h.at[source], sc, sd)
        return source

    def finish(sc, src, dst):
        lanes = pl.ds(pl.multiple_of(sc * part, part), part)
        dst[:, lanes] = src[pl.ds(sc * n_dp, n_dp)].reshape(part, n).T

    for dc in range(n_ctx):
        for dd in range(0, n_dp, 2):
            if (dc, dd) != (0, 0):
                source = h_arrived(*behind(dc, dd))
                push(h_in.at[source], h_in.at[source], send_f.at[source], recv_h.at[source], ctx, sib)
    for dc in range(n_ctx):
        sc, _ = behind(dc, 0)
        for dd in range(n_dp):
            if (dc, dd) != (0, 0):
                _, sd = behind(dc, dd)
                source = sc * n_dp + sd
                arrived(dx_out.at[0, 0], dx_in.at[source], send_dx.at[me], recv_dx.at[source], sc, sd)
        finish(sc, dx_in, dx_ref)
    for dc in range(n_ctx):
        for dd in range(1, n_dp, 2):
            h_arrived(*behind(dc, dd))
        finish(behind(dc, 0)[0], h_in, h_ref)
    for c in sent:
        c.wait_send()


def fused_body(n_ctx, n_dp, grad_out, inputs, filt):
    n, width = filt.shape
    group = n_ctx * n_dp
    cb = width // group
    high, low = half_step_table(n)
    bf16, f32 = jnp.bfloat16, jnp.float32
    sems = pltpu.SemaphoreType.DMA
    hbm_spec = pl.BlockSpec(memory_space=pltpu.HBM)
    vmem_spec = pl.BlockSpec(memory_space=pltpu.VMEM)
    dx, h = pl.pallas_call(
        functools.partial(kernel, n_ctx, n_dp),
        out_shape=(
            jax.ShapeDtypeStruct((n, width), bf16),
            jax.ShapeDtypeStruct((n, width), f32),
        ),
        in_specs=[hbm_spec] * 5,
        out_specs=(vmem_spec, vmem_spec),
        scratch_shapes=[
            pltpu.VMEM((n, width), bf16),
            pltpu.VMEM((n, width), bf16),
            pltpu.VMEM((n, width), bf16),
            pltpu.VMEM((n, 2 * n), bf16),
            pltpu.VMEM((n, 2 * n), bf16),
            pltpu.VMEM((2, group, cb, n), bf16),
            pltpu.VMEM((group, cb, n), bf16),
            pltpu.VMEM((2, n_ctx, n_dp, cb, n), bf16),
            pltpu.VMEM((n_ctx, cb, n), bf16),
            pltpu.VMEM((2, n_ctx, n_dp, cb, 2 * n), f32),
            pltpu.VMEM((n_ctx, cb, 2 * n), f32),
            pltpu.VMEM((n_ctx * cb + group * cb, 2 * n), bf16),
            pltpu.VMEM((n_ctx * cb + group * cb, 2 * n), bf16),
            pltpu.VMEM((n_ctx, cb, n), f32),
            pltpu.VMEM((n_ctx, n_dp, cb, n), bf16),
            pltpu.VMEM((group, cb, n), f32),
            pltpu.VMEM((group, cb, n), bf16),
            sems((5,)),
            sems((2, group)), sems((2, group)),
            sems((n_ctx,)), sems((n_ctx,)),
            sems((group,)), sems((group,)), sems((group,)),
            sems((group,)), sems((group,)),
        ],
        compiler_params=pltpu.CompilerParams(
            collective_id=0, has_side_effects=True, vmem_limit_bytes=40 * 1024 * 1024
        ),
    )(*(
        pltpu.with_memory_space_constraint(a, pltpu.HBM)
        for a in (
            grad_out.reshape(n, width), inputs.reshape(n, width), filt,
            jnp.asarray(high), jnp.asarray(low),
        )
    ))
    return dx.reshape(grad_out.shape), h


full_turn = 2.0 * math.pi


def rotation(left_idx, right_idx, modulus):
    angle = (left_idx * right_idx % modulus).astype(jnp.float32) * (full_turn / modulus)
    return (jnp.cos(angle), jnp.sin(angle))


def contract(form, table, values):
    return jnp.einsum(
        form, table, values, precision=lax.Precision.HIGHEST, preferred_element_type=jnp.float32
    )


def first_section(part, cos_first, sin_first, cos_twist, sin_twist, members, piece_rows):
    values = part.astype(jnp.float32)
    values = values.reshape(values.shape[0], members, piece_rows, values.shape[2])
    real_part = contract("fn,knbc->kfbc", cos_first, values)
    imag_part = -contract("fn,knbc->kfbc", sin_first, values)
    cos_wide = cos_twist[None, :, :, None]
    sin_wide = sin_twist[None, :, :, None]
    return jnp.stack(
        [real_part * cos_wide + imag_part * sin_wide, imag_part * cos_wide - real_part * sin_wide]
    )


def second_section(mixed, cos_second, sin_second):
    real_in = mixed[0]
    imag_in = mixed[1]
    real_out = contract("fn,kgnc->kgfc", cos_second, real_in) + contract(
        "fn,kgnc->kgfc", sin_second, imag_in
    )
    imag_out = contract("fn,kgnc->kgfc", cos_second, imag_in) - contract(
        "fn,kgnc->kgfc", sin_second, real_in
    )
    return (real_out, imag_out)


def body(grad_out, inputs, filt):
    members = lax.axis_size("context")
    position = lax.axis_index("context")
    seq_rows = grad_out.shape[1]
    piece_rows = seq_rows // members
    spread = 2 * members
    modulus = spread * seq_rows
    freq_first = jnp.arange(spread, dtype=jnp.int32)
    dev_first = jnp.arange(members, dtype=jnp.int32)
    cos_first, sin_first = rotation(freq_first[:, None], dev_first[None, :], spread)
    local_rows = position * piece_rows + jnp.arange(piece_rows, dtype=jnp.int32)
    cos_twist, sin_twist = rotation(freq_first[:, None], local_rows[None, :], modulus)
    all_rows = jnp.arange(seq_rows, dtype=jnp.int32)
    cos_second, sin_second = rotation(all_rows[:, None], all_rows[None, :], seq_rows)
    signals = jnp.concatenate([grad_out, inputs], axis=0)
    replicas = lax.axis_size("dp")
    width = filt.shape[1] // replicas
    own_filter = lax.dynamic_slice_in_dim(filt, lax.axis_index("dp") * width, width, 1)[None]
    column_sig, column_filt = (
        lax.all_to_all(signals, "context", split_axis=1, concat_axis=1, tiled=True),
        lax.all_to_all(own_filter, "context", split_axis=1, concat_axis=1, tiled=True),
    )
    sectioned_sig = first_section(
        column_sig, cos_first, sin_first, cos_twist, sin_twist, members, piece_rows
    )
    sectioned_filt = first_section(
        column_filt, cos_first, sin_first, cos_twist, sin_twist, members, piece_rows
    )
    mixed_sig, mixed_filt = (
        lax.all_to_all(sectioned_sig, "context", split_axis=2, concat_axis=3, tiled=True),
        lax.all_to_all(sectioned_filt, "context", split_axis=2, concat_axis=3, tiled=True),
    )
    sig_re, sig_im = second_section(mixed_sig, cos_second, sin_second)
    filt_re, filt_im = second_section(mixed_filt, cos_second, sin_second)
    filt_re, filt_im = (
        lax.all_gather(filt_re, "dp", axis=3, tiled=True),
        lax.all_gather(filt_im, "dp", axis=3, tiled=True),
    )
    grad_re = sig_re[0]
    grad_im = sig_im[0]
    input_re = sig_re[1]
    input_im = sig_im[1]
    kernel_re = filt_re[0]
    kernel_im = filt_im[0]
    dx_re = grad_re * kernel_re + grad_im * kernel_im
    dx_im = grad_im * kernel_re - grad_re * kernel_im
    dh_re = grad_re * input_re + grad_im * input_im
    dh_im = grad_im * input_re - grad_re * input_im
    spec_re = jnp.stack([dx_re, dh_re])
    spec_im = jnp.stack([dx_im, dh_im])
    back_re = contract("nf,sgfc->sgnc", cos_second, spec_re) - contract(
        "nf,sgfc->sgnc", sin_second, spec_im
    )
    back_im = contract("nf,sgfc->sgnc", cos_second, spec_im) + contract(
        "nf,sgfc->sgnc", sin_second, spec_re
    )
    own_freq = 2 * position + jnp.arange(2, dtype=jnp.int32)
    cos_back, sin_back = rotation(own_freq[:, None], all_rows[None, :], modulus)
    cos_wide = cos_back[None, :, :, None]
    sin_wide = sin_back[None, :, :, None]
    turned = jnp.stack(
        [back_re * cos_wide - back_im * sin_wide, back_im * cos_wide + back_re * sin_wide]
    )
    regrouped = lax.all_to_all(turned, "context", split_axis=3, concat_axis=2, tiled=True)
    in_time = contract("fn,sfbc->snbc", cos_first, regrouped[0]) - contract(
        "fn,sfbc->snbc", sin_first, regrouped[1]
    )
    in_time = in_time * (1.0 / modulus)
    restored = lax.all_to_all(in_time, "context", split_axis=1, concat_axis=2, tiled=True)
    input_grad = restored[0].astype(jnp.bfloat16)
    filter_grad = lax.psum(restored[1, 0], "dp")
    return (input_grad, filter_grad)


def any_body(n_ctx, n_dp, grad_out, inputs, filt):
    n, width = filt.shape
    tile = 32
    fits = (
        n_ctx == 2
        and grad_out.shape[0] == 1
        and n_dp % 2 == 0
        and n % 256 == 0
        and width % (n_ctx * n_dp * tile) == 0
        and width % (n_ctx * 128) == 0
        and 16 * n * (n + width) * 4 <= 40 * 1024 * 1024
    )
    if fits:
        return fused_body(n_ctx, n_dp, grad_out, inputs, filt)
    return body(grad_out, inputs, filt)


def solution(mesh):
    return jax.shard_map(
        functools.partial(any_body, mesh.shape["context"], mesh.shape["dp"]),
        mesh=mesh,
        in_specs=(
            P("dp", "context", "tensor"),
            P("dp", "context", "tensor"),
            P("context", "tensor"),
        ),
        out_specs=(P("dp", "context", "tensor"), P("context", "tensor")),
        check_vma=False,
    )
```

```python
import functools
import math

import jax
import jax.numpy as jnp
import ml_dtypes
import numpy as np
from jax import lax
from jax.experimental import pallas as pl
from jax.experimental.pallas import tpu as pltpu
from jax.sharding import PartitionSpec as P

MESH = pl.DeviceIdType.MESH
NT = (((1,), (1,)), ((), ()))


def half_step_table(n):
    k = np.concatenate([np.arange(0, n, 2), np.arange(1, n, 2)])
    turns = (np.arange(n)[:, None] * (2 * k[None, :] + 1)) % (4 * n)
    angle = turns * (math.pi / (2 * n))
    table = np.concatenate([np.cos(angle), -np.sin(angle)], axis=1)
    high = table.astype(ml_dtypes.bfloat16)
    low = (table - high.astype(np.float64)).astype(ml_dtypes.bfloat16)
    return high, low


def dot(a, b):
    return jnp.dot(a, b, preferred_element_type=jnp.float32)


def dot_nt(a, b):
    return lax.dot_general(a, b, NT, preferred_element_type=jnp.float32)


def corr(fr, fi, gr, gi):
    return fr * gr + fi * gi, fr * gi - fi * gr


def kernel(
    n_ctx, n_dp,
    g_hbm, x_hbm, f_hbm, wh_hbm, wl_hbm,
    dx_ref, h_ref,
    g_in, x_in, f_in, wh, wl,
    out1, outf, in1, inf, spec, specf, s_hi, s_lo, h_out, dx_out, h_in, dx_in,
    load_sem, send1, recv1, sendf, recvf, send_h, recv_h, recv_f, send_dx, recv_dx,
):
    n, width = g_hbm.shape
    group = n_ctx * n_dp
    cb = width // group
    half_lanes = n // 2
    ctx = lax.axis_index("context")
    dp = lax.axis_index("dp")
    me = ctx * n_dp + dp

    barrier = pltpu.get_barrier_semaphore()
    offsets = [(dc, dd) for dc in range(n_ctx - 1, -1, -1) for dd in range(n_dp - 1, -1, -1)]
    remote = [o for o in offsets if o != (0, 0)]

    def ahead(dc, dd):
        return lax.rem(ctx + dc, n_ctx), lax.rem(dp + dd, n_dp)

    def behind(dc, dd):
        return lax.rem(ctx + n_ctx - dc, n_ctx), lax.rem(dp + n_dp - dd, n_dp)

    for o in remote:
        pc, pd = ahead(*o)
        pl.semaphore_signal(barrier, inc=1, device_id={"context": pc, "dp": pd}, device_id_type=MESH)
    loads = [
        pltpu.make_async_copy(src, dst, load_sem.at[i])
        for i, (src, dst) in enumerate(
            [(g_hbm, g_in), (x_hbm, x_in), (f_hbm, f_in), (wh_hbm, wh), (wl_hbm, wl)]
        )
    ]
    for c in loads:
        c.start()

    sib = dp + 1 - 2 * lax.rem(dp, 2)

    def push(src, dst, send, recv, pc, pd):
        c = pltpu.make_async_remote_copy(
            src_ref=src, dst_ref=dst, send_sem=send, recv_sem=recv,
            device_id={"context": pc, "dp": pd}, device_id_type=MESH,
        )
        c.start()

    def waiter(ref, sem):
        return pltpu.make_async_remote_copy(
            src_ref=ref, dst_ref=ref, send_sem=sem, recv_sem=sem,
            device_id={"context": ctx, "dp": sib}, device_id_type=MESH,
        )

    def arrived(ref, sem):
        waiter(ref, sem).wait_recv()

    def left(ref, sem):
        waiter(ref, sem).wait_send()

    part = n_dp * cb

    def turn(src, c):
        lanes = pl.ds(pl.multiple_of(c * part, part), part)
        return src[:, lanes].T.reshape(n_dp, cb, n)

    def spread_out(sig, src, dc):
        pc, _ = ahead(dc, 0)
        out1[sig, pl.ds(pc * n_dp, n_dp)] = turn(src, pc)
        if sig == 0 and dc == n_ctx - 1:
            pl.semaphore_wait(barrier, group - 1)
        for dd in range(n_dp - 1, -1, -1):
            if (dc, dd) != (0, 0):
                _, pd = ahead(dc, dd)
                push(
                    out1.at[sig, pc * n_dp + pd], in1.at[sig, ctx, dp],
                    send1.at[sig], recv1.at[sig, ctx], pc, pd,
                )

    loads[0].wait()
    for dc in range(n_ctx - 1, 0, -1):
        spread_out(0, g_in, dc)
    loads[2].wait()
    for dc in range(n_ctx - 1, 0, -1):
        pc, _ = ahead(dc, 0)
        outf[pl.ds(pc * n_dp, n_dp)] = turn(f_in, pc)
        push(outf.at[pc * n_dp + dp], inf.at[ctx], sendf.at[dc], recvf.at[ctx], pc, dp)
    spread_out(0, g_in, 0)
    loads[1].wait()
    for dc in range(n_ctx - 1, -1, -1):
        spread_out(1, x_in, dc)
    outf[pl.ds(ctx * n_dp, n_dp)] = turn(f_in, ctx)
    in1[0, ctx, dp] = out1[0, me]
    in1[1, ctx, dp] = out1[1, me]
    inf[ctx] = outf[me]
    loads[3].wait()
    loads[4].wait()

    def collect(sig, dc):
        sc, _ = behind(dc, 0)
        count = n_dp if dc else n_dp - 1
        arrived(in1.at[sig, sc, pl.ds(0, count)], recv1.at[sig, sc])
        rows = in1[sig, sc].reshape(part, n)
        spec[sig, sc] = (dot(rows, wh[...]) + dot(rows, wl[...])).reshape(n_dp, cb, 2 * n)

    def put(row, lanes, value):
        high = value.astype(jnp.bfloat16)
        s_hi[pl.ds(row, cb), lanes] = high
        s_lo[pl.ds(row, cb), lanes] = (value - high.astype(jnp.float32)).astype(jnp.bfloat16)

    def shifted(parity, b, re, im):
        g0r, g0i = spec[0, 0, b, :, re], spec[0, 0, b, :, im]
        g1r, g1i = spec[0, 1, b, :, re], spec[0, 1, b, :, im]
        if parity == 0:
            return g0r + g1i, g0i - g1r, g1r, g1i
        return g0r - g1i, g0i + g1r, g1r, g1i

    def lanes_of(parity):
        return pl.ds(parity * half_lanes, half_lanes), pl.ds(n + parity * half_lanes, half_lanes)

    def inverse(start, size):
        rows = pl.ds(start, size)
        high, low = s_hi[rows, :], s_lo[rows, :]
        total = dot_nt(high, wh[...]) + (dot_nt(low, wh[...]) + dot_nt(high, wl[...]))
        return total * (1.0 / n)

    collect(0, 0)
    for dc in range(1, n_ctx):
        sc, _ = behind(dc, 0)
        arrived(inf.at[sc], recvf.at[sc])
    rows_f = inf[...].reshape(n_ctx * cb, n)
    specf[...] = (dot(rows_f, wh[...]) + dot(rows_f, wl[...])).reshape(specf.shape)
    for dc in range(1, n_ctx):
        collect(0, dc)
    first = n_ctx * cb
    for parity in range(2):
        re, im = lanes_of(parity)
        f0r, f0i = specf[0, :, re], specf[0, :, im]
        f1r, f1i = specf[1, :, re], specf[1, :, im]
        for b in range(n_dp):
            qr, qi, g1r, g1i = shifted(parity, b, re, im)
            ar, ai = corr(f0r, f0i, qr, qi)
            br, bi = corr(f1r, f1i, g1r, g1i)
            cr, ci = corr(f0r, f0i, g1r, g1i)
            row = first + b * cb
            put(row, re, ar + br)
            put(row, im, ai + bi)
            put(row + part, re, cr)
            put(row + part, im, ci)
    for dc in range(n_ctx - 1, -1, -1):
        pc, _ = ahead(dc, 0)
        start = pl.multiple_of(first + pc * part, cb)
        dx_out[pc] = inverse(start, part).astype(jnp.bfloat16).reshape(n_dp, cb, n)
        for dd in range(n_dp - 1, -1, -1):
            if (dc, dd) != (0, 0):
                _, pd = ahead(dc, dd)
                push(dx_out.at[pc, pd], dx_in.at[me], send_dx.at[0], recv_dx.at[ctx], pc, pd)
    dx_in[me] = dx_out[ctx, dp]

    for dc in range(n_ctx):
        collect(1, dc)
    for parity in range(2):
        re, im = lanes_of(parity)
        h0r = h0i = h1r = h1i = jnp.zeros((cb, half_lanes), jnp.float32)
        for b in range(n_dp):
            qr, qi, g1r, g1i = shifted(parity, b, re, im)
            x0r, x0i = spec[1, 0, b, :, re], spec[1, 0, b, :, im]
            x1r, x1i = spec[1, 1, b, :, re], spec[1, 1, b, :, im]
            ar, ai = corr(x0r, x0i, qr, qi)
            br, bi = corr(x1r, x1i, g1r, g1i)
            cr, ci = corr(x0r, x0i, g1r, g1i)
            h0r, h0i = h0r + (ar + br), h0i + (ai + bi)
            h1r, h1i = h1r + cr, h1i + ci
        put(0, re, h0r)
        put(0, im, h0i)
        put(cb, re, h1r)
        put(cb, im, h1i)
    h_out[...] = inverse(0, n_ctx * cb).reshape(h_out.shape)
    for dc, dd in remote:
        if dd % 2 == 0:
            pc, pd = ahead(dc, dd)
            push(h_out.at[pc], h_in.at[me], send_h.at[0], recv_h.at[ctx, dd // 2], pc, pd)
    push(h_out.at[ctx], h_in.at[me], send_h.at[0], recv_f.at[ctx], ctx, sib)
    h_in[me] = h_out[ctx]

    def finish(sc, src, dst):
        lanes = pl.ds(pl.multiple_of(sc * part, part), part)
        dst[:, lanes] = src[pl.ds(sc * n_dp, n_dp)].reshape(part, n).T

    for dc in range(n_ctx):
        for dd in range(0, n_dp, 2):
            if (dc, dd) != (0, 0):
                sc, sd = behind(dc, dd)
                source = sc * n_dp + sd
                arrived(h_in.at[source], recv_h.at[sc, dd // 2])
                push(h_in.at[source], h_in.at[source], send_h.at[0], recv_f.at[sc], ctx, sib)
    for dc in range(n_ctx):
        sc, _ = behind(dc, 0)
        count = n_dp if dc else n_dp - 1
        arrived(dx_in.at[pl.ds(0, count)], recv_dx.at[sc])
        finish(sc, dx_in, dx_ref)
    for dc in range(n_ctx):
        sc, _ = behind(dc, 0)
        arrived(h_in.at[pl.ds(0, n_dp // 2)], recv_f.at[sc])
        finish(sc, h_in, h_ref)
    for sig in range(2):
        left(out1.at[sig, pl.ds(0, group - 1)], send1.at[sig])
    for dc in range(1, n_ctx):
        left(inf.at[0], sendf.at[dc])
    left(dx_in.at[pl.ds(0, group - 1)], send_dx.at[0])
    left(h_in.at[pl.ds(0, group - 1)], send_h.at[0])


def write_out(dx_src, h_src, dx_ref, h_ref, sem):
    copies = [
        pltpu.make_async_copy(h_src, h_ref, sem.at[0]),
        pltpu.make_async_copy(dx_src, dx_ref, sem.at[1]),
    ]
    for c in copies:
        c.start()
    for c in copies:
        c.wait()


def fused_body(n_ctx, n_dp, grad_out, inputs, filt):
    n, width = filt.shape
    group = n_ctx * n_dp
    cb = width // group
    high, low = half_step_table(n)
    bf16, f32 = jnp.bfloat16, jnp.float32
    sems = pltpu.SemaphoreType.DMA
    hbm_spec = pl.BlockSpec(memory_space=pltpu.HBM)
    vmem_spec = pl.BlockSpec(memory_space=pltpu.VMEM)
    dx, h = pl.pallas_call(
        functools.partial(kernel, n_ctx, n_dp),
        out_shape=(
            jax.ShapeDtypeStruct((n, width), bf16),
            jax.ShapeDtypeStruct((n, width), f32),
        ),
        in_specs=[hbm_spec] * 5,
        out_specs=(vmem_spec, vmem_spec),
        scratch_shapes=[
            pltpu.VMEM((n, width), bf16),
            pltpu.VMEM((n, width), bf16),
            pltpu.VMEM((n, width), bf16),
            pltpu.VMEM((n, 2 * n), bf16),
            pltpu.VMEM((n, 2 * n), bf16),
            pltpu.VMEM((2, group, cb, n), bf16),
            pltpu.VMEM((group, cb, n), bf16),
            pltpu.VMEM((2, n_ctx, n_dp, cb, n), bf16),
            pltpu.VMEM((n_ctx, cb, n), bf16),
            pltpu.VMEM((2, n_ctx, n_dp, cb, 2 * n), f32),
            pltpu.VMEM((n_ctx, cb, 2 * n), f32),
            pltpu.VMEM((n_ctx * cb + group * cb, 2 * n), bf16),
            pltpu.VMEM((n_ctx * cb + group * cb, 2 * n), bf16),
            pltpu.VMEM((n_ctx, cb, n), f32),
            pltpu.VMEM((n_ctx, n_dp, cb, n), bf16),
            pltpu.VMEM((group, cb, n), f32),
            pltpu.VMEM((group, cb, n), bf16),
            sems((5,)),
            sems((2,)), sems((2, n_ctx)),
            sems((n_ctx,)), sems((n_ctx,)),
            sems((1,)), sems((n_ctx, n_dp // 2)), sems((n_ctx,)),
            sems((1,)), sems((n_ctx,)),
        ],
        compiler_params=pltpu.CompilerParams(
            collective_id=0, has_side_effects=True, vmem_limit_bytes=40 * 1024 * 1024
        ),
    )(*(
        pltpu.with_memory_space_constraint(a, pltpu.HBM)
        for a in (
            grad_out.reshape(n, width), inputs.reshape(n, width), filt,
            jnp.asarray(high), jnp.asarray(low),
        )
    ))
    dx, h = pl.pallas_call(
        write_out,
        out_shape=(pltpu.HBM((n, width), bf16), pltpu.HBM((n, width), f32)),
        in_specs=[pl.BlockSpec(memory_space=pl.ANY)] * 2,
        out_specs=(hbm_spec, hbm_spec),
        scratch_shapes=[sems((2,))],
    )(dx, h)
    return dx.reshape(grad_out.shape), h


full_turn = 2.0 * math.pi


def rotation(left_idx, right_idx, modulus):
    angle = (left_idx * right_idx % modulus).astype(jnp.float32) * (full_turn / modulus)
    return (jnp.cos(angle), jnp.sin(angle))


def contract(form, table, values):
    return jnp.einsum(
        form, table, values, precision=lax.Precision.HIGHEST, preferred_element_type=jnp.float32
    )


def first_section(part, cos_first, sin_first, cos_twist, sin_twist, members, piece_rows):
    values = part.astype(jnp.float32)
    values = values.reshape(values.shape[0], members, piece_rows, values.shape[2])
    real_part = contract("fn,knbc->kfbc", cos_first, values)
    imag_part = -contract("fn,knbc->kfbc", sin_first, values)
    cos_wide = cos_twist[None, :, :, None]
    sin_wide = sin_twist[None, :, :, None]
    return jnp.stack(
        [real_part * cos_wide + imag_part * sin_wide, imag_part * cos_wide - real_part * sin_wide]
    )


def second_section(mixed, cos_second, sin_second):
    real_in = mixed[0]
    imag_in = mixed[1]
    real_out = contract("fn,kgnc->kgfc", cos_second, real_in) + contract(
        "fn,kgnc->kgfc", sin_second, imag_in
    )
    imag_out = contract("fn,kgnc->kgfc", cos_second, imag_in) - contract(
        "fn,kgnc->kgfc", sin_second, real_in
    )
    return (real_out, imag_out)


def body(grad_out, inputs, filt):
    members = lax.axis_size("context")
    position = lax.axis_index("context")
    seq_rows = grad_out.shape[1]
    piece_rows = seq_rows // members
    spread = 2 * members
    modulus = spread * seq_rows
    freq_first = jnp.arange(spread, dtype=jnp.int32)
    dev_first = jnp.arange(members, dtype=jnp.int32)
    cos_first, sin_first = rotation(freq_first[:, None], dev_first[None, :], spread)
    local_rows = position * piece_rows + jnp.arange(piece_rows, dtype=jnp.int32)
    cos_twist, sin_twist = rotation(freq_first[:, None], local_rows[None, :], modulus)
    all_rows = jnp.arange(seq_rows, dtype=jnp.int32)
    cos_second, sin_second = rotation(all_rows[:, None], all_rows[None, :], seq_rows)
    signals = jnp.concatenate([grad_out, inputs], axis=0)
    replicas = lax.axis_size("dp")
    width = filt.shape[1] // replicas
    own_filter = lax.dynamic_slice_in_dim(filt, lax.axis_index("dp") * width, width, 1)[None]
    column_sig, column_filt = (
        lax.all_to_all(signals, "context", split_axis=1, concat_axis=1, tiled=True),
        lax.all_to_all(own_filter, "context", split_axis=1, concat_axis=1, tiled=True),
    )
    sectioned_sig = first_section(
        column_sig, cos_first, sin_first, cos_twist, sin_twist, members, piece_rows
    )
    sectioned_filt = first_section(
        column_filt, cos_first, sin_first, cos_twist, sin_twist, members, piece_rows
    )
    mixed_sig, mixed_filt = (
        lax.all_to_all(sectioned_sig, "context", split_axis=2, concat_axis=3, tiled=True),
        lax.all_to_all(sectioned_filt, "context", split_axis=2, concat_axis=3, tiled=True),
    )
    sig_re, sig_im = second_section(mixed_sig, cos_second, sin_second)
    filt_re, filt_im = second_section(mixed_filt, cos_second, sin_second)
    filt_re, filt_im = (
        lax.all_gather(filt_re, "dp", axis=3, tiled=True),
        lax.all_gather(filt_im, "dp", axis=3, tiled=True),
    )
    grad_re = sig_re[0]
    grad_im = sig_im[0]
    input_re = sig_re[1]
    input_im = sig_im[1]
    kernel_re = filt_re[0]
    kernel_im = filt_im[0]
    dx_re = grad_re * kernel_re + grad_im * kernel_im
    dx_im = grad_im * kernel_re - grad_re * kernel_im
    dh_re = grad_re * input_re + grad_im * input_im
    dh_im = grad_im * input_re - grad_re * input_im
    spec_re = jnp.stack([dx_re, dh_re])
    spec_im = jnp.stack([dx_im, dh_im])
    back_re = contract("nf,sgfc->sgnc", cos_second, spec_re) - contract(
        "nf,sgfc->sgnc", sin_second, spec_im
    )
    back_im = contract("nf,sgfc->sgnc", cos_second, spec_im) + contract(
        "nf,sgfc->sgnc", sin_second, spec_re
    )
    own_freq = 2 * position + jnp.arange(2, dtype=jnp.int32)
    cos_back, sin_back = rotation(own_freq[:, None], all_rows[None, :], modulus)
    cos_wide = cos_back[None, :, :, None]
    sin_wide = sin_back[None, :, :, None]
    turned = jnp.stack(
        [back_re * cos_wide - back_im * sin_wide, back_im * cos_wide + back_re * sin_wide]
    )
    regrouped = lax.all_to_all(turned, "context", split_axis=3, concat_axis=2, tiled=True)
    in_time = contract("fn,sfbc->snbc", cos_first, regrouped[0]) - contract(
        "fn,sfbc->snbc", sin_first, regrouped[1]
    )
    in_time = in_time * (1.0 / modulus)
    restored = lax.all_to_all(in_time, "context", split_axis=1, concat_axis=2, tiled=True)
    input_grad = restored[0].astype(jnp.bfloat16)
    filter_grad = lax.psum(restored[1, 0], "dp")
    return (input_grad, filter_grad)


def any_body(n_ctx, n_dp, grad_out, inputs, filt):
    n, width = filt.shape
    tile = 32
    fits = (
        n_ctx == 2
        and grad_out.shape[0] == 1
        and n_dp % 2 == 0
        and n % 256 == 0
        and width % (n_ctx * n_dp * tile) == 0
        and width % (n_ctx * 128) == 0
        and 16 * n * (n + width) * 4 <= 40 * 1024 * 1024
    )
    if fits:
        return fused_body(n_ctx, n_dp, grad_out, inputs, filt)
    return body(grad_out, inputs, filt)


def solution(mesh):
    return jax.shard_map(
        functools.partial(any_body, mesh.shape["context"], mesh.shape["dp"]),
        mesh=mesh,
        in_specs=(
            P("dp", "context", "tensor"),
            P("dp", "context", "tensor"),
            P("context", "tensor"),
        ),
        out_specs=(P("dp", "context", "tensor"), P("context", "tensor")),
        check_vma=False,
    )
```

```python
import functools
import math

import jax
import jax.numpy as jnp
import ml_dtypes
import numpy as np
from jax import lax
from jax.experimental import pallas as pl
from jax.experimental.pallas import tpu as pltpu
from jax.sharding import PartitionSpec as P

MESH = pl.DeviceIdType.MESH


def half_step_table(n):
    k = np.concatenate([np.arange(0, n, 2), np.arange(1, n, 2)])
    turns = (np.arange(n)[:, None] * (2 * k[None, :] + 1)) % (4 * n)
    angle = turns * (math.pi / (2 * n))
    table = np.concatenate([np.cos(angle), -np.sin(angle)], axis=1)
    high = table.astype(ml_dtypes.bfloat16)
    low = (table - high.astype(np.float64)).astype(ml_dtypes.bfloat16)
    return high, low


def dot(a, b):
    return jnp.dot(a, b, preferred_element_type=jnp.float32)


def corr(fr, fi, gr, gi):
    return fr * gr + fi * gi, fr * gi - fi * gr


def kernel(
    n_ctx, n_dp,
    g_hbm, x_hbm, f_hbm, wh_hbm, wl_hbm, vh_hbm, vl_hbm,
    dx_ref, h_ref,
    g_in, x_in, f_in, wh, wl, vh, vl,
    out1, outf, in1, inf, spec, specf, s_hi, s_lo, h_out, dx_out, h_in, dx_in,
    load_sem, send1, recv1, sendf, recvf, send_h, recv_h, recv_f, send_dx, recv_dx,
):
    n, width = g_hbm.shape
    group = n_ctx * n_dp
    cb = width // group
    half_lanes = n // 2
    ctx = lax.axis_index("context")
    dp = lax.axis_index("dp")
    me = ctx * n_dp + dp

    barrier = pltpu.get_barrier_semaphore()
    offsets = [(dc, dd) for dc in range(n_ctx - 1, -1, -1) for dd in range(n_dp - 1, -1, -1)]
    remote = [o for o in offsets if o != (0, 0)]

    def ahead(dc, dd):
        return lax.rem(ctx + dc, n_ctx), lax.rem(dp + dd, n_dp)

    def behind(dc, dd):
        return lax.rem(ctx + n_ctx - dc, n_ctx), lax.rem(dp + n_dp - dd, n_dp)

    for o in remote:
        pc, pd = ahead(*o)
        pl.semaphore_signal(barrier, inc=1, device_id={"context": pc, "dp": pd}, device_id_type=MESH)
    loads = [
        pltpu.make_async_copy(src, dst, load_sem.at[i])
        for i, (src, dst) in enumerate(
            [
                (g_hbm, g_in), (x_hbm, x_in), (f_hbm, f_in), (wh_hbm, wh), (wl_hbm, wl),
                (vh_hbm, vh), (vl_hbm, vl),
            ]
        )
    ]
    for c in loads:
        c.start()

    sib = dp + 1 - 2 * lax.rem(dp, 2)

    def push(src, dst, send, recv, pc, pd):
        c = pltpu.make_async_remote_copy(
            src_ref=src, dst_ref=dst, send_sem=send, recv_sem=recv,
            device_id={"context": pc, "dp": pd}, device_id_type=MESH,
        )
        c.start()

    def waiter(ref, sem):
        return pltpu.make_async_remote_copy(
            src_ref=ref, dst_ref=ref, send_sem=sem, recv_sem=sem,
            device_id={"context": ctx, "dp": sib}, device_id_type=MESH,
        )

    def arrived(ref, sem):
        waiter(ref, sem).wait_recv()

    def left(ref, sem):
        waiter(ref, sem).wait_send()

    part = n_dp * cb

    def turn(src, c):
        lanes = pl.ds(pl.multiple_of(c * part, part), part)
        return src[:, lanes].T.reshape(n_dp, cb, n)

    def spread_out(sig, src, dc):
        pc, _ = ahead(dc, 0)
        out1[sig, pl.ds(pc * n_dp, n_dp)] = turn(src, pc)
        if sig == 0 and dc == n_ctx - 1:
            pl.semaphore_wait(barrier, group - 1)
        for dd in range(n_dp - 1, -1, -1):
            if (dc, dd) != (0, 0):
                _, pd = ahead(dc, dd)
                push(
                    out1.at[sig, pc * n_dp + pd], in1.at[sig, ctx, dp],
                    send1.at[sig], recv1.at[sig, ctx], pc, pd,
                )

    loads[0].wait()
    for dc in range(n_ctx - 1, 0, -1):
        spread_out(0, g_in, dc)
    loads[2].wait()
    for dc in range(n_ctx - 1, 0, -1):
        pc, _ = ahead(dc, 0)
        outf[pl.ds(pc * n_dp, n_dp)] = turn(f_in, pc)
        push(outf.at[pc * n_dp + dp], inf.at[ctx], sendf.at[dc], recvf.at[ctx], pc, dp)
    spread_out(0, g_in, 0)
    loads[1].wait()
    for dc in range(n_ctx - 1, -1, -1):
        spread_out(1, x_in, dc)
    outf[pl.ds(ctx * n_dp, n_dp)] = turn(f_in, ctx)
    in1[0, ctx, dp] = out1[0, me]
    in1[1, ctx, dp] = out1[1, me]
    inf[ctx] = outf[me]
    loads[3].wait()
    loads[4].wait()
    loads[5].wait()
    loads[6].wait()

    def collect(sig, dc):
        sc, _ = behind(dc, 0)
        count = n_dp if dc else n_dp - 1
        arrived(in1.at[sig, sc, pl.ds(0, count)], recv1.at[sig, sc])
        rows = in1[sig, sc].reshape(part, n)
        spec[sig, sc] = (dot(rows, wh[...]) + dot(rows, wl[...])).reshape(n_dp, cb, 2 * n)

    def put(row, lanes, value):
        high = value.astype(jnp.bfloat16)
        s_hi[pl.ds(row, cb), lanes] = high
        s_lo[pl.ds(row, cb), lanes] = (value - high.astype(jnp.float32)).astype(jnp.bfloat16)

    def shifted(parity, b, re, im):
        g0r, g0i = spec[0, 0, b, :, re], spec[0, 0, b, :, im]
        g1r, g1i = spec[0, 1, b, :, re], spec[0, 1, b, :, im]
        if parity == 0:
            return g0r + g1i, g0i - g1r, g1r, g1i
        return g0r - g1i, g0i + g1r, g1r, g1i

    def lanes_of(parity):
        return pl.ds(parity * half_lanes, half_lanes), pl.ds(n + parity * half_lanes, half_lanes)

    def inverse(start, size):
        rows = pl.ds(start, size)
        high, low = s_hi[rows, :], s_lo[rows, :]
        total = dot(high, vh[...]) + (dot(low, vh[...]) + dot(high, vl[...]))
        return total * (1.0 / n)

    collect(0, 0)
    for dc in range(1, n_ctx):
        sc, _ = behind(dc, 0)
        arrived(inf.at[sc], recvf.at[sc])
    rows_f = inf[...].reshape(n_ctx * cb, n)
    specf[...] = (dot(rows_f, wh[...]) + dot(rows_f, wl[...])).reshape(specf.shape)
    for dc in range(1, n_ctx):
        collect(0, dc)
    first = n_ctx * cb
    for parity in range(2):
        re, im = lanes_of(parity)
        f0r, f0i = specf[0, :, re], specf[0, :, im]
        f1r, f1i = specf[1, :, re], specf[1, :, im]
        for b in range(n_dp):
            qr, qi, g1r, g1i = shifted(parity, b, re, im)
            ar, ai = corr(f0r, f0i, qr, qi)
            br, bi = corr(f1r, f1i, g1r, g1i)
            cr, ci = corr(f0r, f0i, g1r, g1i)
            row = first + b * cb
            put(row, re, ar + br)
            put(row, im, ai + bi)
            put(row + part, re, cr)
            put(row + part, im, ci)
    for dc in range(n_ctx - 1, -1, -1):
        pc, _ = ahead(dc, 0)
        start = pl.multiple_of(first + pc * part, cb)
        dx_out[pc] = inverse(start, part).astype(jnp.bfloat16).reshape(n_dp, cb, n)
        for dd in range(n_dp - 1, -1, -1):
            if (dc, dd) != (0, 0):
                _, pd = ahead(dc, dd)
                push(dx_out.at[pc, pd], dx_in.at[me], send_dx.at[0], recv_dx.at[ctx], pc, pd)
    dx_in[me] = dx_out[ctx, dp]

    for dc in range(n_ctx):
        collect(1, dc)
    for parity in range(2):
        re, im = lanes_of(parity)
        h0r = h0i = h1r = h1i = jnp.zeros((cb, half_lanes), jnp.float32)
        for b in range(n_dp):
            qr, qi, g1r, g1i = shifted(parity, b, re, im)
            x0r, x0i = spec[1, 0, b, :, re], spec[1, 0, b, :, im]
            x1r, x1i = spec[1, 1, b, :, re], spec[1, 1, b, :, im]
            ar, ai = corr(x0r, x0i, qr, qi)
            br, bi = corr(x1r, x1i, g1r, g1i)
            cr, ci = corr(x0r, x0i, g1r, g1i)
            h0r, h0i = h0r + (ar + br), h0i + (ai + bi)
            h1r, h1i = h1r + cr, h1i + ci
        put(0, re, h0r)
        put(0, im, h0i)
        put(cb, re, h1r)
        put(cb, im, h1i)
    h_out[...] = inverse(0, n_ctx * cb).reshape(h_out.shape)
    for dc, dd in remote:
        if dd % 2 == 0:
            pc, pd = ahead(dc, dd)
            push(h_out.at[pc], h_in.at[me], send_h.at[0], recv_h.at[ctx, dd // 2], pc, pd)
    push(h_out.at[ctx], h_in.at[me], send_h.at[0], recv_f.at[ctx], ctx, sib)
    h_in[me] = h_out[ctx]

    def finish(sc, src, dst):
        lanes = pl.ds(pl.multiple_of(sc * part, part), part)
        dst[:, lanes] = src[pl.ds(sc * n_dp, n_dp)].reshape(part, n).T

    for dc in range(n_ctx):
        for dd in range(0, n_dp, 2):
            if (dc, dd) != (0, 0):
                sc, sd = behind(dc, dd)
                source = sc * n_dp + sd
                arrived(h_in.at[source], recv_h.at[sc, dd // 2])
                push(h_in.at[source], h_in.at[source], send_h.at[0], recv_f.at[sc], ctx, sib)
    for dc in range(n_ctx):
        sc, _ = behind(dc, 0)
        count = n_dp if dc else n_dp - 1
        arrived(dx_in.at[pl.ds(0, count)], recv_dx.at[sc])
        finish(sc, dx_in, dx_ref)
    for dc in range(n_ctx):
        sc, _ = behind(dc, 0)
        arrived(h_in.at[pl.ds(0, n_dp // 2)], recv_f.at[sc])
        finish(sc, h_in, h_ref)
    for sig in range(2):
        left(out1.at[sig, pl.ds(0, group - 1)], send1.at[sig])
    for dc in range(1, n_ctx):
        left(inf.at[0], sendf.at[dc])
    left(dx_in.at[pl.ds(0, group - 1)], send_dx.at[0])
    left(h_in.at[pl.ds(0, group - 1)], send_h.at[0])


def write_out(dx_src, h_src, dx_ref, h_ref, sem):
    copies = [
        pltpu.make_async_copy(h_src, h_ref, sem.at[0]),
        pltpu.make_async_copy(dx_src, dx_ref, sem.at[1]),
    ]
    for c in copies:
        c.start()
    for c in copies:
        c.wait()


def fused_body(n_ctx, n_dp, grad_out, inputs, filt):
    n, width = filt.shape
    group = n_ctx * n_dp
    cb = width // group
    high, low = half_step_table(n)
    bf16, f32 = jnp.bfloat16, jnp.float32
    sems = pltpu.SemaphoreType.DMA
    hbm_spec = pl.BlockSpec(memory_space=pltpu.HBM)
    vmem_spec = pl.BlockSpec(memory_space=pltpu.VMEM)
    dx, h = pl.pallas_call(
        functools.partial(kernel, n_ctx, n_dp),
        out_shape=(
            jax.ShapeDtypeStruct((n, width), bf16),
            jax.ShapeDtypeStruct((n, width), f32),
        ),
        in_specs=[hbm_spec] * 7,
        out_specs=(vmem_spec, vmem_spec),
        scratch_shapes=[
            pltpu.VMEM((n, width), bf16),
            pltpu.VMEM((n, width), bf16),
            pltpu.VMEM((n, width), bf16),
            pltpu.VMEM((n, 2 * n), bf16),
            pltpu.VMEM((n, 2 * n), bf16),
            pltpu.VMEM((2 * n, n), bf16),
            pltpu.VMEM((2 * n, n), bf16),
            pltpu.VMEM((2, group, cb, n), bf16),
            pltpu.VMEM((group, cb, n), bf16),
            pltpu.VMEM((2, n_ctx, n_dp, cb, n), bf16),
            pltpu.VMEM((n_ctx, cb, n), bf16),
            pltpu.VMEM((2, n_ctx, n_dp, cb, 2 * n), f32),
            pltpu.VMEM((n_ctx, cb, 2 * n), f32),
            pltpu.VMEM((n_ctx * cb + group * cb, 2 * n), bf16),
            pltpu.VMEM((n_ctx * cb + group * cb, 2 * n), bf16),
            pltpu.VMEM((n_ctx, cb, n), f32),
            pltpu.VMEM((n_ctx, n_dp, cb, n), bf16),
            pltpu.VMEM((group, cb, n), f32),
            pltpu.VMEM((group, cb, n), bf16),
            sems((7,)),
            sems((2,)), sems((2, n_ctx)),
            sems((n_ctx,)), sems((n_ctx,)),
            sems((1,)), sems((n_ctx, n_dp // 2)), sems((n_ctx,)),
            sems((1,)), sems((n_ctx,)),
        ],
        compiler_params=pltpu.CompilerParams(
            collective_id=0, has_side_effects=True, vmem_limit_bytes=40 * 1024 * 1024
        ),
    )(*(
        pltpu.with_memory_space_constraint(a, pltpu.HBM)
        for a in (
            grad_out.reshape(n, width), inputs.reshape(n, width), filt,
            jnp.asarray(high), jnp.asarray(low),
            jnp.asarray(np.ascontiguousarray(high.T)), jnp.asarray(np.ascontiguousarray(low.T)),
        )
    ))
    dx, h = pl.pallas_call(
        write_out,
        out_shape=(pltpu.HBM((n, width), bf16), pltpu.HBM((n, width), f32)),
        in_specs=[pl.BlockSpec(memory_space=pl.ANY)] * 2,
        out_specs=(hbm_spec, hbm_spec),
        scratch_shapes=[sems((2,))],
        compiler_params=pltpu.CompilerParams(vmem_limit_bytes=4 * 1024 * 1024),
    )(dx, h)
    return dx.reshape(grad_out.shape), h


full_turn = 2.0 * math.pi


def rotation(left_idx, right_idx, modulus):
    angle = (left_idx * right_idx % modulus).astype(jnp.float32) * (full_turn / modulus)
    return (jnp.cos(angle), jnp.sin(angle))


def contract(form, table, values):
    return jnp.einsum(
        form, table, values, precision=lax.Precision.HIGHEST, preferred_element_type=jnp.float32
    )


def first_section(part, cos_first, sin_first, cos_twist, sin_twist, members, piece_rows):
    values = part.astype(jnp.float32)
    values = values.reshape(values.shape[0], members, piece_rows, values.shape[2])
    real_part = contract("fn,knbc->kfbc", cos_first, values)
    imag_part = -contract("fn,knbc->kfbc", sin_first, values)
    cos_wide = cos_twist[None, :, :, None]
    sin_wide = sin_twist[None, :, :, None]
    return jnp.stack(
        [real_part * cos_wide + imag_part * sin_wide, imag_part * cos_wide - real_part * sin_wide]
    )


def second_section(mixed, cos_second, sin_second):
    real_in = mixed[0]
    imag_in = mixed[1]
    real_out = contract("fn,kgnc->kgfc", cos_second, real_in) + contract(
        "fn,kgnc->kgfc", sin_second, imag_in
    )
    imag_out = contract("fn,kgnc->kgfc", cos_second, imag_in) - contract(
        "fn,kgnc->kgfc", sin_second, real_in
    )
    return (real_out, imag_out)


def body(grad_out, inputs, filt):
    members = lax.axis_size("context")
    position = lax.axis_index("context")
    seq_rows = grad_out.shape[1]
    piece_rows = seq_rows // members
    spread = 2 * members
    modulus = spread * seq_rows
    freq_first = jnp.arange(spread, dtype=jnp.int32)
    dev_first = jnp.arange(members, dtype=jnp.int32)
    cos_first, sin_first = rotation(freq_first[:, None], dev_first[None, :], spread)
    local_rows = position * piece_rows + jnp.arange(piece_rows, dtype=jnp.int32)
    cos_twist, sin_twist = rotation(freq_first[:, None], local_rows[None, :], modulus)
    all_rows = jnp.arange(seq_rows, dtype=jnp.int32)
    cos_second, sin_second = rotation(all_rows[:, None], all_rows[None, :], seq_rows)
    signals = jnp.concatenate([grad_out, inputs], axis=0)
    replicas = lax.axis_size("dp")
    width = filt.shape[1] // replicas
    own_filter = lax.dynamic_slice_in_dim(filt, lax.axis_index("dp") * width, width, 1)[None]
    column_sig, column_filt = (
        lax.all_to_all(signals, "context", split_axis=1, concat_axis=1, tiled=True),
        lax.all_to_all(own_filter, "context", split_axis=1, concat_axis=1, tiled=True),
    )
    sectioned_sig = first_section(
        column_sig, cos_first, sin_first, cos_twist, sin_twist, members, piece_rows
    )
    sectioned_filt = first_section(
        column_filt, cos_first, sin_first, cos_twist, sin_twist, members, piece_rows
    )
    mixed_sig, mixed_filt = (
        lax.all_to_all(sectioned_sig, "context", split_axis=2, concat_axis=3, tiled=True),
        lax.all_to_all(sectioned_filt, "context", split_axis=2, concat_axis=3, tiled=True),
    )
    sig_re, sig_im = second_section(mixed_sig, cos_second, sin_second)
    filt_re, filt_im = second_section(mixed_filt, cos_second, sin_second)
    filt_re, filt_im = (
        lax.all_gather(filt_re, "dp", axis=3, tiled=True),
        lax.all_gather(filt_im, "dp", axis=3, tiled=True),
    )
    grad_re = sig_re[0]
    grad_im = sig_im[0]
    input_re = sig_re[1]
    input_im = sig_im[1]
    kernel_re = filt_re[0]
    kernel_im = filt_im[0]
    dx_re = grad_re * kernel_re + grad_im * kernel_im
    dx_im = grad_im * kernel_re - grad_re * kernel_im
    dh_re = grad_re * input_re + grad_im * input_im
    dh_im = grad_im * input_re - grad_re * input_im
    spec_re = jnp.stack([dx_re, dh_re])
    spec_im = jnp.stack([dx_im, dh_im])
    back_re = contract("nf,sgfc->sgnc", cos_second, spec_re) - contract(
        "nf,sgfc->sgnc", sin_second, spec_im
    )
    back_im = contract("nf,sgfc->sgnc", cos_second, spec_im) + contract(
        "nf,sgfc->sgnc", sin_second, spec_re
    )
    own_freq = 2 * position + jnp.arange(2, dtype=jnp.int32)
    cos_back, sin_back = rotation(own_freq[:, None], all_rows[None, :], modulus)
    cos_wide = cos_back[None, :, :, None]
    sin_wide = sin_back[None, :, :, None]
    turned = jnp.stack(
        [back_re * cos_wide - back_im * sin_wide, back_im * cos_wide + back_re * sin_wide]
    )
    regrouped = lax.all_to_all(turned, "context", split_axis=3, concat_axis=2, tiled=True)
    in_time = contract("fn,sfbc->snbc", cos_first, regrouped[0]) - contract(
        "fn,sfbc->snbc", sin_first, regrouped[1]
    )
    in_time = in_time * (1.0 / modulus)
    restored = lax.all_to_all(in_time, "context", split_axis=1, concat_axis=2, tiled=True)
    input_grad = restored[0].astype(jnp.bfloat16)
    filter_grad = lax.psum(restored[1, 0], "dp")
    return (input_grad, filter_grad)


def any_body(n_ctx, n_dp, grad_out, inputs, filt):
    n, width = filt.shape
    tile = 32
    fits = (
        n_ctx == 2
        and grad_out.shape[0] == 1
        and n_dp % 2 == 0
        and n % 256 == 0
        and width % (n_ctx * n_dp * tile) == 0
        and width % (n_ctx * 128) == 0
        and 16 * n * (n + width) * 4 <= 40 * 1024 * 1024
    )
    if fits:
        return fused_body(n_ctx, n_dp, grad_out, inputs, filt)
    return body(grad_out, inputs, filt)


def solution(mesh):
    return jax.shard_map(
        functools.partial(any_body, mesh.shape["context"], mesh.shape["dp"]),
        mesh=mesh,
        in_specs=(
            P("dp", "context", "tensor"),
            P("dp", "context", "tensor"),
            P("context", "tensor"),
        ),
        out_specs=(P("dp", "context", "tensor"), P("context", "tensor")),
        check_vma=False,
    )
```

```python
import functools
import math

import jax
import jax.numpy as jnp
import ml_dtypes
import numpy as np
from jax import lax
from jax.experimental import pallas as pl
from jax.experimental.pallas import tpu as pltpu
from jax.sharding import PartitionSpec as P

MESH = pl.DeviceIdType.MESH


def half_step_table(n):
    k = np.concatenate([np.arange(0, n, 2), np.arange(1, n, 2)])
    turns = (np.arange(n)[:, None] * (2 * k[None, :] + 1)) % (4 * n)
    angle = turns * (math.pi / (2 * n))
    table = np.concatenate([np.cos(angle), -np.sin(angle)], axis=1)
    high = table.astype(ml_dtypes.bfloat16)
    low = (table - high.astype(np.float64)).astype(ml_dtypes.bfloat16)
    return high, low


def dot(a, b):
    return jnp.dot(a, b, preferred_element_type=jnp.float32)


def corr(fr, fi, gr, gi):
    return fr * gr + fi * gi, fr * gi - fi * gr


def kernel(
    n_ctx, n_dp,
    g_hbm, x_hbm, f_hbm, wh_hbm, wl_hbm, vh_hbm, vl_hbm,
    dx_ref, h_ref,
    g_in, x_in, f_in, wh, wl, vh, vl,
    out1, outf, in1, inf, spec, specf, s_hi, s_lo, h_out, dx_out, h_in, dx_in,
    load_sem, send1, recv1, sendf, recvf, send_h, recv_h, recv_f, send_dx, recv_dx,
):
    n, width = g_hbm.shape
    group = n_ctx * n_dp
    cb = width // group
    half_lanes = n // 2
    ctx = lax.axis_index("context")
    dp = lax.axis_index("dp")
    me = ctx * n_dp + dp

    barrier = pltpu.get_barrier_semaphore()
    offsets = [(dc, dd) for dc in range(n_ctx - 1, -1, -1) for dd in range(n_dp - 1, -1, -1)]
    remote = [o for o in offsets if o != (0, 0)]

    def ahead(dc, dd):
        return lax.rem(ctx + dc, n_ctx), lax.rem(dp + dd, n_dp)

    def behind(dc, dd):
        return lax.rem(ctx + n_ctx - dc, n_ctx), lax.rem(dp + n_dp - dd, n_dp)

    for o in remote:
        pc, pd = ahead(*o)
        pl.semaphore_signal(barrier, inc=1, device_id={"context": pc, "dp": pd}, device_id_type=MESH)
    loads = [
        pltpu.make_async_copy(src, dst, load_sem.at[i])
        for i, (src, dst) in enumerate(
            [
                (g_hbm, g_in), (x_hbm, x_in), (f_hbm, f_in), (wh_hbm, wh), (wl_hbm, wl),
                (vh_hbm, vh), (vl_hbm, vl),
            ]
        )
    ]
    for c in loads:
        c.start()

    sib = dp + 1 - 2 * lax.rem(dp, 2)

    def push(src, dst, send, recv, pc, pd):
        c = pltpu.make_async_remote_copy(
            src_ref=src, dst_ref=dst, send_sem=send, recv_sem=recv,
            device_id={"context": pc, "dp": pd}, device_id_type=MESH,
        )
        c.start()

    def waiter(ref, sem):
        return pltpu.make_async_remote_copy(
            src_ref=ref, dst_ref=ref, send_sem=sem, recv_sem=sem,
            device_id={"context": ctx, "dp": sib}, device_id_type=MESH,
        )

    def arrived(ref, sem):
        waiter(ref, sem).wait_recv()

    def left(ref, sem):
        waiter(ref, sem).wait_send()

    part = n_dp * cb

    def turn(src, c):
        lanes = pl.ds(pl.multiple_of(c * part, part), part)
        return src[:, lanes].T.reshape(n_dp, cb, n)

    loads[0].wait()
    loads[1].wait()
    for dc in range(n_ctx - 1, -1, -1):
        pc, _ = ahead(dc, 0)
        blocks = pl.ds(pc * n_dp, n_dp)
        out1[blocks, 0] = turn(g_in, pc)
        out1[blocks, 1] = turn(x_in, pc)
        if dc == n_ctx - 1:
            pl.semaphore_wait(barrier, group - 1)
        for dd in range(n_dp - 1, -1, -1):
            if (dc, dd) != (0, 0):
                _, pd = ahead(dc, dd)
                push(
                    out1.at[pc * n_dp + pd], in1.at[ctx, dp],
                    send1.at[0], recv1.at[ctx], pc, pd,
                )
    loads[2].wait()
    for dc in range(n_ctx - 1, 0, -1):
        pc, _ = ahead(dc, 0)
        outf[pl.ds(pc * n_dp, n_dp)] = turn(f_in, pc)
        push(outf.at[pc * n_dp + dp], inf.at[ctx], sendf.at[dc], recvf.at[ctx], pc, dp)
    outf[pl.ds(ctx * n_dp, n_dp)] = turn(f_in, ctx)
    in1[ctx, dp] = out1[me]
    inf[ctx] = outf[me]
    loads[3].wait()
    loads[4].wait()
    loads[5].wait()
    loads[6].wait()

    def collect(dc):
        sc, _ = behind(dc, 0)
        count = n_dp if dc else n_dp - 1
        arrived(in1.at[sc, pl.ds(0, count)], recv1.at[sc])
        rows = in1[sc].reshape(2 * part, n)
        spec[sc] = (dot(rows, wh[...]) + dot(rows, wl[...])).reshape(n_dp, 2, cb, 2 * n)

    def put(row, lanes, value):
        high = value.astype(jnp.bfloat16)
        s_hi[pl.ds(row, cb), lanes] = high
        s_lo[pl.ds(row, cb), lanes] = (value - high.astype(jnp.float32)).astype(jnp.bfloat16)

    def shifted(parity, b, re, im):
        g0r, g0i = spec[0, b, 0, :, re], spec[0, b, 0, :, im]
        g1r, g1i = spec[1, b, 0, :, re], spec[1, b, 0, :, im]
        if parity == 0:
            return g0r + g1i, g0i - g1r, g1r, g1i
        return g0r - g1i, g0i + g1r, g1r, g1i

    def lanes_of(parity):
        return pl.ds(parity * half_lanes, half_lanes), pl.ds(n + parity * half_lanes, half_lanes)

    def inverse(start, size):
        rows = pl.ds(start, size)
        high, low = s_hi[rows, :], s_lo[rows, :]
        total = dot(high, vh[...]) + (dot(low, vh[...]) + dot(high, vl[...]))
        return total * (1.0 / n)

    for dc in range(n_ctx):
        collect(dc)
    for parity in range(2):
        re, im = lanes_of(parity)
        h0r = h0i = h1r = h1i = jnp.zeros((cb, half_lanes), jnp.float32)
        for b in range(n_dp):
            qr, qi, g1r, g1i = shifted(parity, b, re, im)
            x0r, x0i = spec[0, b, 1, :, re], spec[0, b, 1, :, im]
            x1r, x1i = spec[1, b, 1, :, re], spec[1, b, 1, :, im]
            ar, ai = corr(x0r, x0i, qr, qi)
            br, bi = corr(x1r, x1i, g1r, g1i)
            cr, ci = corr(x0r, x0i, g1r, g1i)
            h0r, h0i = h0r + (ar + br), h0i + (ai + bi)
            h1r, h1i = h1r + cr, h1i + ci
        put(0, re, h0r)
        put(0, im, h0i)
        put(cb, re, h1r)
        put(cb, im, h1i)
    h_out[...] = inverse(0, n_ctx * cb).reshape(h_out.shape)
    for dc, dd in remote:
        if dd % 2 == 0:
            pc, pd = ahead(dc, dd)
            push(h_out.at[pc], h_in.at[me], send_h.at[0], recv_h.at[ctx, dd // 2], pc, pd)
    push(h_out.at[ctx], h_in.at[me], send_h.at[0], recv_f.at[ctx], ctx, sib)
    h_in[me] = h_out[ctx]

    for dc in range(1, n_ctx):
        sc, _ = behind(dc, 0)
        arrived(inf.at[sc], recvf.at[sc])
    rows_f = inf[...].reshape(n_ctx * cb, n)
    specf[...] = (dot(rows_f, wh[...]) + dot(rows_f, wl[...])).reshape(specf.shape)
    first = n_ctx * cb
    for parity in range(2):
        re, im = lanes_of(parity)
        f0r, f0i = specf[0, :, re], specf[0, :, im]
        f1r, f1i = specf[1, :, re], specf[1, :, im]
        for b in range(n_dp):
            qr, qi, g1r, g1i = shifted(parity, b, re, im)
            ar, ai = corr(f0r, f0i, qr, qi)
            br, bi = corr(f1r, f1i, g1r, g1i)
            cr, ci = corr(f0r, f0i, g1r, g1i)
            row = first + b * cb
            put(row, re, ar + br)
            put(row, im, ai + bi)
            put(row + part, re, cr)
            put(row + part, im, ci)
    for dc in range(n_ctx - 1, -1, -1):
        pc, _ = ahead(dc, 0)
        start = pl.multiple_of(first + pc * part, cb)
        dx_out[pc] = inverse(start, part).astype(jnp.bfloat16).reshape(n_dp, cb, n)
        for dd in range(n_dp - 1, -1, -1):
            if (dc, dd) != (0, 0):
                _, pd = ahead(dc, dd)
                push(dx_out.at[pc, pd], dx_in.at[me], send_dx.at[0], recv_dx.at[ctx], pc, pd)
    dx_in[me] = dx_out[ctx, dp]

    def finish(sc, src, dst):
        lanes = pl.ds(pl.multiple_of(sc * part, part), part)
        dst[:, lanes] = src[pl.ds(sc * n_dp, n_dp)].reshape(part, n).T

    for dc in range(n_ctx):
        for dd in range(0, n_dp, 2):
            if (dc, dd) != (0, 0):
                sc, sd = behind(dc, dd)
                source = sc * n_dp + sd
                arrived(h_in.at[source], recv_h.at[sc, dd // 2])
                push(h_in.at[source], h_in.at[source], send_h.at[0], recv_f.at[sc], ctx, sib)
    for dc in range(n_ctx):
        sc, _ = behind(dc, 0)
        count = n_dp if dc else n_dp - 1
        arrived(dx_in.at[pl.ds(0, count)], recv_dx.at[sc])
        finish(sc, dx_in, dx_ref)
    for dc in range(n_ctx):
        sc, _ = behind(dc, 0)
        arrived(h_in.at[pl.ds(0, n_dp // 2)], recv_f.at[sc])
        finish(sc, h_in, h_ref)
    left(out1.at[pl.ds(0, group - 1)], send1.at[0])
    for dc in range(1, n_ctx):
        left(inf.at[0], sendf.at[dc])
    left(dx_in.at[pl.ds(0, group - 1)], send_dx.at[0])
    left(h_in.at[pl.ds(0, group - 1)], send_h.at[0])


def write_out(dx_src, h_src, dx_ref, h_ref, sem):
    copies = [
        pltpu.make_async_copy(h_src, h_ref, sem.at[0]),
        pltpu.make_async_copy(dx_src, dx_ref, sem.at[1]),
    ]
    for c in copies:
        c.start()
    for c in copies:
        c.wait()


def fused_body(n_ctx, n_dp, grad_out, inputs, filt):
    n, width = filt.shape
    group = n_ctx * n_dp
    cb = width // group
    high, low = half_step_table(n)
    bf16, f32 = jnp.bfloat16, jnp.float32
    sems = pltpu.SemaphoreType.DMA
    hbm_spec = pl.BlockSpec(memory_space=pltpu.HBM)
    vmem_spec = pl.BlockSpec(memory_space=pltpu.VMEM)
    dx, h = pl.pallas_call(
        functools.partial(kernel, n_ctx, n_dp),
        out_shape=(
            jax.ShapeDtypeStruct((n, width), bf16),
            jax.ShapeDtypeStruct((n, width), f32),
        ),
        in_specs=[hbm_spec] * 7,
        out_specs=(vmem_spec, vmem_spec),
        scratch_shapes=[
            pltpu.VMEM((n, width), bf16),
            pltpu.VMEM((n, width), bf16),
            pltpu.VMEM((n, width), bf16),
            pltpu.VMEM((n, 2 * n), bf16),
            pltpu.VMEM((n, 2 * n), bf16),
            pltpu.VMEM((2 * n, n), bf16),
            pltpu.VMEM((2 * n, n), bf16),
            pltpu.VMEM((group, 2, cb, n), bf16),
            pltpu.VMEM((group, cb, n), bf16),
            pltpu.VMEM((n_ctx, n_dp, 2, cb, n), bf16),
            pltpu.VMEM((n_ctx, cb, n), bf16),
            pltpu.VMEM((n_ctx, n_dp, 2, cb, 2 * n), f32),
            pltpu.VMEM((n_ctx, cb, 2 * n), f32),
            pltpu.VMEM((n_ctx * cb + group * cb, 2 * n), bf16),
            pltpu.VMEM((n_ctx * cb + group * cb, 2 * n), bf16),
            pltpu.VMEM((n_ctx, cb, n), f32),
            pltpu.VMEM((n_ctx, n_dp, cb, n), bf16),
            pltpu.VMEM((group, cb, n), f32),
            pltpu.VMEM((group, cb, n), bf16),
            sems((7,)),
            sems((1,)), sems((n_ctx,)),
            sems((n_ctx,)), sems((n_ctx,)),
            sems((1,)), sems((n_ctx, n_dp // 2)), sems((n_ctx,)),
            sems((1,)), sems((n_ctx,)),
        ],
        compiler_params=pltpu.CompilerParams(
            collective_id=0, has_side_effects=True, vmem_limit_bytes=40 * 1024 * 1024
        ),
    )(*(
        pltpu.with_memory_space_constraint(a, pltpu.HBM)
        for a in (
            grad_out.reshape(n, width), inputs.reshape(n, width), filt,
            jnp.asarray(high), jnp.asarray(low),
            jnp.asarray(np.ascontiguousarray(high.T)), jnp.asarray(np.ascontiguousarray(low.T)),
        )
    ))
    dx, h = pl.pallas_call(
        write_out,
        out_shape=(pltpu.HBM((n, width), bf16), pltpu.HBM((n, width), f32)),
        in_specs=[pl.BlockSpec(memory_space=pl.ANY)] * 2,
        out_specs=(hbm_spec, hbm_spec),
        scratch_shapes=[sems((2,))],
        compiler_params=pltpu.CompilerParams(vmem_limit_bytes=4 * 1024 * 1024),
    )(dx, h)
    return dx.reshape(grad_out.shape), h


full_turn = 2.0 * math.pi


def rotation(left_idx, right_idx, modulus):
    angle = (left_idx * right_idx % modulus).astype(jnp.float32) * (full_turn / modulus)
    return (jnp.cos(angle), jnp.sin(angle))


def contract(form, table, values):
    return jnp.einsum(
        form, table, values, precision=lax.Precision.HIGHEST, preferred_element_type=jnp.float32
    )


def first_section(part, cos_first, sin_first, cos_twist, sin_twist, members, piece_rows):
    values = part.astype(jnp.float32)
    values = values.reshape(values.shape[0], members, piece_rows, values.shape[2])
    real_part = contract("fn,knbc->kfbc", cos_first, values)
    imag_part = -contract("fn,knbc->kfbc", sin_first, values)
    cos_wide = cos_twist[None, :, :, None]
    sin_wide = sin_twist[None, :, :, None]
    return jnp.stack(
        [real_part * cos_wide + imag_part * sin_wide, imag_part * cos_wide - real_part * sin_wide]
    )


def second_section(mixed, cos_second, sin_second):
    real_in = mixed[0]
    imag_in = mixed[1]
    real_out = contract("fn,kgnc->kgfc", cos_second, real_in) + contract(
        "fn,kgnc->kgfc", sin_second, imag_in
    )
    imag_out = contract("fn,kgnc->kgfc", cos_second, imag_in) - contract(
        "fn,kgnc->kgfc", sin_second, real_in
    )
    return (real_out, imag_out)


def body(grad_out, inputs, filt):
    members = lax.axis_size("context")
    position = lax.axis_index("context")
    seq_rows = grad_out.shape[1]
    piece_rows = seq_rows // members
    spread = 2 * members
    modulus = spread * seq_rows
    freq_first = jnp.arange(spread, dtype=jnp.int32)
    dev_first = jnp.arange(members, dtype=jnp.int32)
    cos_first, sin_first = rotation(freq_first[:, None], dev_first[None, :], spread)
    local_rows = position * piece_rows + jnp.arange(piece_rows, dtype=jnp.int32)
    cos_twist, sin_twist = rotation(freq_first[:, None], local_rows[None, :], modulus)
    all_rows = jnp.arange(seq_rows, dtype=jnp.int32)
    cos_second, sin_second = rotation(all_rows[:, None], all_rows[None, :], seq_rows)
    signals = jnp.concatenate([grad_out, inputs], axis=0)
    replicas = lax.axis_size("dp")
    width = filt.shape[1] // replicas
    own_filter = lax.dynamic_slice_in_dim(filt, lax.axis_index("dp") * width, width, 1)[None]
    column_sig, column_filt = (
        lax.all_to_all(signals, "context", split_axis=1, concat_axis=1, tiled=True),
        lax.all_to_all(own_filter, "context", split_axis=1, concat_axis=1, tiled=True),
    )
    sectioned_sig = first_section(
        column_sig, cos_first, sin_first, cos_twist, sin_twist, members, piece_rows
    )
    sectioned_filt = first_section(
        column_filt, cos_first, sin_first, cos_twist, sin_twist, members, piece_rows
    )
    mixed_sig, mixed_filt = (
        lax.all_to_all(sectioned_sig, "context", split_axis=2, concat_axis=3, tiled=True),
        lax.all_to_all(sectioned_filt, "context", split_axis=2, concat_axis=3, tiled=True),
    )
    sig_re, sig_im = second_section(mixed_sig, cos_second, sin_second)
    filt_re, filt_im = second_section(mixed_filt, cos_second, sin_second)
    filt_re, filt_im = (
        lax.all_gather(filt_re, "dp", axis=3, tiled=True),
        lax.all_gather(filt_im, "dp", axis=3, tiled=True),
    )
    grad_re = sig_re[0]
    grad_im = sig_im[0]
    input_re = sig_re[1]
    input_im = sig_im[1]
    kernel_re = filt_re[0]
    kernel_im = filt_im[0]
    dx_re = grad_re * kernel_re + grad_im * kernel_im
    dx_im = grad_im * kernel_re - grad_re * kernel_im
    dh_re = grad_re * input_re + grad_im * input_im
    dh_im = grad_im * input_re - grad_re * input_im
    spec_re = jnp.stack([dx_re, dh_re])
    spec_im = jnp.stack([dx_im, dh_im])
    back_re = contract("nf,sgfc->sgnc", cos_second, spec_re) - contract(
        "nf,sgfc->sgnc", sin_second, spec_im
    )
    back_im = contract("nf,sgfc->sgnc", cos_second, spec_im) + contract(
        "nf,sgfc->sgnc", sin_second, spec_re
    )
    own_freq = 2 * position + jnp.arange(2, dtype=jnp.int32)
    cos_back, sin_back = rotation(own_freq[:, None], all_rows[None, :], modulus)
    cos_wide = cos_back[None, :, :, None]
    sin_wide = sin_back[None, :, :, None]
    turned = jnp.stack(
        [back_re * cos_wide - back_im * sin_wide, back_im * cos_wide + back_re * sin_wide]
    )
    regrouped = lax.all_to_all(turned, "context", split_axis=3, concat_axis=2, tiled=True)
    in_time = contract("fn,sfbc->snbc", cos_first, regrouped[0]) - contract(
        "fn,sfbc->snbc", sin_first, regrouped[1]
    )
    in_time = in_time * (1.0 / modulus)
    restored = lax.all_to_all(in_time, "context", split_axis=1, concat_axis=2, tiled=True)
    input_grad = restored[0].astype(jnp.bfloat16)
    filter_grad = lax.psum(restored[1, 0], "dp")
    return (input_grad, filter_grad)


def any_body(n_ctx, n_dp, grad_out, inputs, filt):
    n, width = filt.shape
    tile = 32
    fits = (
        n_ctx == 2
        and grad_out.shape[0] == 1
        and n_dp % 2 == 0
        and n % 256 == 0
        and width % (n_ctx * n_dp * tile) == 0
        and width % (n_ctx * 128) == 0
        and 16 * n * (n + width) * 4 <= 40 * 1024 * 1024
    )
    if fits:
        return fused_body(n_ctx, n_dp, grad_out, inputs, filt)
    return body(grad_out, inputs, filt)


def solution(mesh):
    return jax.shard_map(
        functools.partial(any_body, mesh.shape["context"], mesh.shape["dp"]),
        mesh=mesh,
        in_specs=(
            P("dp", "context", "tensor"),
            P("dp", "context", "tensor"),
            P("context", "tensor"),
        ),
        out_specs=(P("dp", "context", "tensor"), P("context", "tensor")),
        check_vma=False,
    )
```

```python
import functools
import math

import jax
import jax.numpy as jnp
import ml_dtypes
import numpy as np
from jax import lax
from jax.experimental import pallas as pl
from jax.experimental.pallas import tpu as pltpu
from jax.sharding import PartitionSpec as P

MESH = pl.DeviceIdType.MESH


def half_step_table(n):
    k = np.concatenate([np.arange(0, n, 2), np.arange(1, n, 2)])
    turns = (np.arange(n)[:, None] * (2 * k[None, :] + 1)) % (4 * n)
    angle = turns * (math.pi / (2 * n))
    table = np.concatenate([np.cos(angle), -np.sin(angle)], axis=1)
    high = table.astype(ml_dtypes.bfloat16)
    low = (table - high.astype(np.float64)).astype(ml_dtypes.bfloat16)
    return high, low


def dot(a, b):
    return jnp.dot(a, b, preferred_element_type=jnp.float32)


def corr(fr, fi, gr, gi):
    return fr * gr + fi * gi, fr * gi - fi * gr


def kernel(
    n_ctx, n_dp,
    g_hbm, x_hbm, f_hbm, wh_hbm, wl_hbm, vh_hbm, vl_hbm,
    dx_ref, h_ref,
    g_in, x_in, f_in, wh, wl, vh, vl,
    out1, outf, in1, inf, spec, specf, s_hi, s_lo, h_out, dx_out, h_in, dx_in,
    load_sem, send1, recv1, sendf, recvf, send_h, recv_h, send_dx, recv_dx,
):
    n, width = g_hbm.shape
    group = n_ctx * n_dp
    cb = width // group
    half_lanes = n // 2
    ctx = lax.axis_index("context")
    dp = lax.axis_index("dp")
    me = ctx * n_dp + dp

    barrier = pltpu.get_barrier_semaphore()
    offsets = [(dc, dd) for dc in range(n_ctx - 1, -1, -1) for dd in range(n_dp - 1, -1, -1)]
    remote = [o for o in offsets if o != (0, 0)]

    def ahead(dc, dd):
        return lax.rem(ctx + dc, n_ctx), lax.rem(dp + dd, n_dp)

    def behind(dc, dd):
        return lax.rem(ctx + n_ctx - dc, n_ctx), lax.rem(dp + n_dp - dd, n_dp)

    for o in remote:
        pc, pd = ahead(*o)
        pl.semaphore_signal(barrier, inc=1, device_id={"context": pc, "dp": pd}, device_id_type=MESH)
    loads = [
        pltpu.make_async_copy(src, dst, load_sem.at[i])
        for i, (src, dst) in enumerate(
            [
                (g_hbm, g_in), (x_hbm, x_in), (f_hbm, f_in), (wh_hbm, wh), (wl_hbm, wl),
                (vh_hbm, vh), (vl_hbm, vl),
            ]
        )
    ]
    for c in loads:
        c.start()

    sib = dp + 1 - 2 * lax.rem(dp, 2)

    def push(src, dst, send, recv, pc, pd):
        c = pltpu.make_async_remote_copy(
            src_ref=src, dst_ref=dst, send_sem=send, recv_sem=recv,
            device_id={"context": pc, "dp": pd}, device_id_type=MESH,
        )
        c.start()

    def waiter(ref, sem):
        return pltpu.make_async_remote_copy(
            src_ref=ref, dst_ref=ref, send_sem=sem, recv_sem=sem,
            device_id={"context": ctx, "dp": sib}, device_id_type=MESH,
        )

    def arrived(ref, sem):
        waiter(ref, sem).wait_recv()

    def left(ref, sem):
        waiter(ref, sem).wait_send()

    part = n_dp * cb

    def turn(src, c):
        lanes = pl.ds(pl.multiple_of(c * part, part), part)
        return src[:, lanes].T.reshape(n_dp, cb, n)

    def spread_out(sig, src, dc):
        pc, _ = ahead(dc, 0)
        out1[sig, pl.ds(pc * n_dp, n_dp)] = turn(src, pc)
        if sig == 0 and dc == n_ctx - 1:
            pl.semaphore_wait(barrier, group - 1)
        for dd in range(n_dp - 1, -1, -1):
            if (dc, dd) != (0, 0):
                _, pd = ahead(dc, dd)
                push(
                    out1.at[sig, pc * n_dp + pd], in1.at[sig, ctx, dp],
                    send1.at[sig], recv1.at[sig, ctx], pc, pd,
                )

    loads[0].wait()
    for dc in range(n_ctx - 1, 0, -1):
        spread_out(0, g_in, dc)
    loads[2].wait()
    for dc in range(n_ctx - 1, 0, -1):
        pc, _ = ahead(dc, 0)
        outf[pl.ds(pc * n_dp, n_dp)] = turn(f_in, pc)
        push(outf.at[pc * n_dp + dp], inf.at[ctx], sendf.at[dc], recvf.at[ctx], pc, dp)
    spread_out(0, g_in, 0)
    loads[1].wait()
    for dc in range(n_ctx - 1, -1, -1):
        spread_out(1, x_in, dc)
    outf[pl.ds(ctx * n_dp, n_dp)] = turn(f_in, ctx)
    in1[0, ctx, dp] = out1[0, me]
    in1[1, ctx, dp] = out1[1, me]
    inf[ctx] = outf[me]
    loads[3].wait()
    loads[4].wait()
    loads[5].wait()
    loads[6].wait()

    def collect(sig, dc):
        sc, _ = behind(dc, 0)
        count = n_dp if dc else n_dp - 1
        arrived(in1.at[sig, sc, pl.ds(0, count)], recv1.at[sig, sc])
        rows = in1[sig, sc].reshape(part, n)
        spec[sig, sc] = (dot(rows, wh[...]) + dot(rows, wl[...])).reshape(n_dp, cb, 2 * n)

    def put(row, lanes, value):
        high = value.astype(jnp.bfloat16)
        s_hi[pl.ds(row, cb), lanes] = high
        s_lo[pl.ds(row, cb), lanes] = (value - high.astype(jnp.float32)).astype(jnp.bfloat16)

    def shifted(parity, b, re, im):
        g0r, g0i = spec[0, 0, b, :, re], spec[0, 0, b, :, im]
        g1r, g1i = spec[0, 1, b, :, re], spec[0, 1, b, :, im]
        if parity == 0:
            return g0r + g1i, g0i - g1r, g1r, g1i
        return g0r - g1i, g0i + g1r, g1r, g1i

    def lanes_of(parity):
        return pl.ds(parity * half_lanes, half_lanes), pl.ds(n + parity * half_lanes, half_lanes)

    def inverse(start, size):
        rows = pl.ds(start, size)
        high, low = s_hi[rows, :], s_lo[rows, :]
        total = dot(high, vh[...]) + (dot(low, vh[...]) + dot(high, vl[...]))
        return total * (1.0 / n)

    collect(0, 0)
    for dc in range(1, n_ctx):
        sc, _ = behind(dc, 0)
        arrived(inf.at[sc], recvf.at[sc])
    rows_f = inf[...].reshape(n_ctx * cb, n)
    specf[...] = (dot(rows_f, wh[...]) + dot(rows_f, wl[...])).reshape(specf.shape)
    for dc in range(1, n_ctx):
        collect(0, dc)
    first = n_ctx * cb
    for parity in range(2):
        re, im = lanes_of(parity)
        f0r, f0i = specf[0, :, re], specf[0, :, im]
        f1r, f1i = specf[1, :, re], specf[1, :, im]
        for b in range(n_dp):
            qr, qi, g1r, g1i = shifted(parity, b, re, im)
            ar, ai = corr(f0r, f0i, qr, qi)
            br, bi = corr(f1r, f1i, g1r, g1i)
            cr, ci = corr(f0r, f0i, g1r, g1i)
            row = first + b * cb
            put(row, re, ar + br)
            put(row, im, ai + bi)
            put(row + part, re, cr)
            put(row + part, im, ci)
    for dc in range(n_ctx - 1, -1, -1):
        pc, _ = ahead(dc, 0)
        start = pl.multiple_of(first + pc * part, cb)
        dx_out[pc] = inverse(start, part).astype(jnp.bfloat16).reshape(n_dp, cb, n)
        for dd in range(n_dp - 1, -1, -1):
            if (dc, dd) != (0, 0):
                _, pd = ahead(dc, dd)
                push(dx_out.at[pc, pd], dx_in.at[me], send_dx.at[0], recv_dx.at[ctx], pc, pd)
    dx_in[me] = dx_out[ctx, dp]

    for dc in range(n_ctx):
        collect(1, dc)
    for parity in range(2):
        re, im = lanes_of(parity)
        h0r = h0i = h1r = h1i = jnp.zeros((cb, half_lanes), jnp.float32)
        for b in range(n_dp):
            qr, qi, g1r, g1i = shifted(parity, b, re, im)
            x0r, x0i = spec[1, 0, b, :, re], spec[1, 0, b, :, im]
            x1r, x1i = spec[1, 1, b, :, re], spec[1, 1, b, :, im]
            ar, ai = corr(x0r, x0i, qr, qi)
            br, bi = corr(x1r, x1i, g1r, g1i)
            cr, ci = corr(x0r, x0i, g1r, g1i)
            h0r, h0i = h0r + (ar + br), h0i + (ai + bi)
            h1r, h1i = h1r + cr, h1i + ci
        put(0, re, h0r)
        put(0, im, h0i)
        put(cb, re, h1r)
        put(cb, im, h1i)
    h_out[...] = inverse(0, n_ctx * cb).reshape(h_out.shape)
    for o in remote:
        pc, pd = ahead(*o)
        push(h_out.at[pc], h_in.at[me], send_h.at[0], recv_h.at[ctx], pc, pd)
    h_in[me] = h_out[ctx]

    def finish(sc, src, dst):
        lanes = pl.ds(pl.multiple_of(sc * part, part), part)
        dst[:, lanes] = src[pl.ds(sc * n_dp, n_dp)].reshape(part, n).T

    for dc in range(n_ctx):
        sc, _ = behind(dc, 0)
        count = n_dp if dc else n_dp - 1
        arrived(dx_in.at[pl.ds(0, count)], recv_dx.at[sc])
        finish(sc, dx_in, dx_ref)
    for dc in range(n_ctx):
        sc, _ = behind(dc, 0)
        count = n_dp if dc else n_dp - 1
        arrived(h_in.at[pl.ds(0, count)], recv_h.at[sc])
        finish(sc, h_in, h_ref)
    for sig in range(2):
        left(out1.at[sig, pl.ds(0, group - 1)], send1.at[sig])
    for dc in range(1, n_ctx):
        left(inf.at[0], sendf.at[dc])
    left(dx_in.at[pl.ds(0, group - 1)], send_dx.at[0])
    left(h_in.at[pl.ds(0, group - 1)], send_h.at[0])


def write_out(dx_src, h_src, dx_ref, h_ref, sem):
    copies = [
        pltpu.make_async_copy(h_src, h_ref, sem.at[0]),
        pltpu.make_async_copy(dx_src, dx_ref, sem.at[1]),
    ]
    for c in copies:
        c.start()
    for c in copies:
        c.wait()


def fused_body(n_ctx, n_dp, grad_out, inputs, filt):
    n, width = filt.shape
    group = n_ctx * n_dp
    cb = width // group
    high, low = half_step_table(n)
    bf16, f32 = jnp.bfloat16, jnp.float32
    sems = pltpu.SemaphoreType.DMA
    hbm_spec = pl.BlockSpec(memory_space=pltpu.HBM)
    vmem_spec = pl.BlockSpec(memory_space=pltpu.VMEM)
    dx, h = pl.pallas_call(
        functools.partial(kernel, n_ctx, n_dp),
        out_shape=(
            jax.ShapeDtypeStruct((n, width), bf16),
            jax.ShapeDtypeStruct((n, width), f32),
        ),
        in_specs=[hbm_spec] * 7,
        out_specs=(vmem_spec, vmem_spec),
        scratch_shapes=[
            pltpu.VMEM((n, width), bf16),
            pltpu.VMEM((n, width), bf16),
            pltpu.VMEM((n, width), bf16),
            pltpu.VMEM((n, 2 * n), bf16),
            pltpu.VMEM((n, 2 * n), bf16),
            pltpu.VMEM((2 * n, n), bf16),
            pltpu.VMEM((2 * n, n), bf16),
            pltpu.VMEM((2, group, cb, n), bf16),
            pltpu.VMEM((group, cb, n), bf16),
            pltpu.VMEM((2, n_ctx, n_dp, cb, n), bf16),
            pltpu.VMEM((n_ctx, cb, n), bf16),
            pltpu.VMEM((2, n_ctx, n_dp, cb, 2 * n), f32),
            pltpu.VMEM((n_ctx, cb, 2 * n), f32),
            pltpu.VMEM((n_ctx * cb + group * cb, 2 * n), bf16),
            pltpu.VMEM((n_ctx * cb + group * cb, 2 * n), bf16),
            pltpu.VMEM((n_ctx, cb, n), f32),
            pltpu.VMEM((n_ctx, n_dp, cb, n), bf16),
            pltpu.VMEM((group, cb, n), f32),
            pltpu.VMEM((group, cb, n), bf16),
            sems((7,)),
            sems((2,)), sems((2, n_ctx)),
            sems((n_ctx,)), sems((n_ctx,)),
            sems((1,)), sems((n_ctx,)),
            sems((1,)), sems((n_ctx,)),
        ],
        compiler_params=pltpu.CompilerParams(
            collective_id=0, has_side_effects=True, vmem_limit_bytes=40 * 1024 * 1024
        ),
    )(*(
        pltpu.with_memory_space_constraint(a, pltpu.HBM)
        for a in (
            grad_out.reshape(n, width), inputs.reshape(n, width), filt,
            jnp.asarray(high), jnp.asarray(low),
            jnp.asarray(np.ascontiguousarray(high.T)), jnp.asarray(np.ascontiguousarray(low.T)),
        )
    ))
    dx, h = pl.pallas_call(
        write_out,
        out_shape=(pltpu.HBM((n, width), bf16), pltpu.HBM((n, width), f32)),
        in_specs=[pl.BlockSpec(memory_space=pl.ANY)] * 2,
        out_specs=(hbm_spec, hbm_spec),
        scratch_shapes=[sems((2,))],
        compiler_params=pltpu.CompilerParams(vmem_limit_bytes=4 * 1024 * 1024),
    )(dx, h)
    return dx.reshape(grad_out.shape), h


full_turn = 2.0 * math.pi


def rotation(left_idx, right_idx, modulus):
    angle = (left_idx * right_idx % modulus).astype(jnp.float32) * (full_turn / modulus)
    return (jnp.cos(angle), jnp.sin(angle))


def contract(form, table, values):
    return jnp.einsum(
        form, table, values, precision=lax.Precision.HIGHEST, preferred_element_type=jnp.float32
    )


def first_section(part, cos_first, sin_first, cos_twist, sin_twist, members, piece_rows):
    values = part.astype(jnp.float32)
    values = values.reshape(values.shape[0], members, piece_rows, values.shape[2])
    real_part = contract("fn,knbc->kfbc", cos_first, values)
    imag_part = -contract("fn,knbc->kfbc", sin_first, values)
    cos_wide = cos_twist[None, :, :, None]
    sin_wide = sin_twist[None, :, :, None]
    return jnp.stack(
        [real_part * cos_wide + imag_part * sin_wide, imag_part * cos_wide - real_part * sin_wide]
    )


def second_section(mixed, cos_second, sin_second):
    real_in = mixed[0]
    imag_in = mixed[1]
    real_out = contract("fn,kgnc->kgfc", cos_second, real_in) + contract(
        "fn,kgnc->kgfc", sin_second, imag_in
    )
    imag_out = contract("fn,kgnc->kgfc", cos_second, imag_in) - contract(
        "fn,kgnc->kgfc", sin_second, real_in
    )
    return (real_out, imag_out)


def body(grad_out, inputs, filt):
    members = lax.axis_size("context")
    position = lax.axis_index("context")
    seq_rows = grad_out.shape[1]
    piece_rows = seq_rows // members
    spread = 2 * members
    modulus = spread * seq_rows
    freq_first = jnp.arange(spread, dtype=jnp.int32)
    dev_first = jnp.arange(members, dtype=jnp.int32)
    cos_first, sin_first = rotation(freq_first[:, None], dev_first[None, :], spread)
    local_rows = position * piece_rows + jnp.arange(piece_rows, dtype=jnp.int32)
    cos_twist, sin_twist = rotation(freq_first[:, None], local_rows[None, :], modulus)
    all_rows = jnp.arange(seq_rows, dtype=jnp.int32)
    cos_second, sin_second = rotation(all_rows[:, None], all_rows[None, :], seq_rows)
    signals = jnp.concatenate([grad_out, inputs], axis=0)
    replicas = lax.axis_size("dp")
    width = filt.shape[1] // replicas
    own_filter = lax.dynamic_slice_in_dim(filt, lax.axis_index("dp") * width, width, 1)[None]
    column_sig, column_filt = (
        lax.all_to_all(signals, "context", split_axis=1, concat_axis=1, tiled=True),
        lax.all_to_all(own_filter, "context", split_axis=1, concat_axis=1, tiled=True),
    )
    sectioned_sig = first_section(
        column_sig, cos_first, sin_first, cos_twist, sin_twist, members, piece_rows
    )
    sectioned_filt = first_section(
        column_filt, cos_first, sin_first, cos_twist, sin_twist, members, piece_rows
    )
    mixed_sig, mixed_filt = (
        lax.all_to_all(sectioned_sig, "context", split_axis=2, concat_axis=3, tiled=True),
        lax.all_to_all(sectioned_filt, "context", split_axis=2, concat_axis=3, tiled=True),
    )
    sig_re, sig_im = second_section(mixed_sig, cos_second, sin_second)
    filt_re, filt_im = second_section(mixed_filt, cos_second, sin_second)
    filt_re, filt_im = (
        lax.all_gather(filt_re, "dp", axis=3, tiled=True),
        lax.all_gather(filt_im, "dp", axis=3, tiled=True),
    )
    grad_re = sig_re[0]
    grad_im = sig_im[0]
    input_re = sig_re[1]
    input_im = sig_im[1]
    kernel_re = filt_re[0]
    kernel_im = filt_im[0]
    dx_re = grad_re * kernel_re + grad_im * kernel_im
    dx_im = grad_im * kernel_re - grad_re * kernel_im
    dh_re = grad_re * input_re + grad_im * input_im
    dh_im = grad_im * input_re - grad_re * input_im
    spec_re = jnp.stack([dx_re, dh_re])
    spec_im = jnp.stack([dx_im, dh_im])
    back_re = contract("nf,sgfc->sgnc", cos_second, spec_re) - contract(
        "nf,sgfc->sgnc", sin_second, spec_im
    )
    back_im = contract("nf,sgfc->sgnc", cos_second, spec_im) + contract(
        "nf,sgfc->sgnc", sin_second, spec_re
    )
    own_freq = 2 * position + jnp.arange(2, dtype=jnp.int32)
    cos_back, sin_back = rotation(own_freq[:, None], all_rows[None, :], modulus)
    cos_wide = cos_back[None, :, :, None]
    sin_wide = sin_back[None, :, :, None]
    turned = jnp.stack(
        [back_re * cos_wide - back_im * sin_wide, back_im * cos_wide + back_re * sin_wide]
    )
    regrouped = lax.all_to_all(turned, "context", split_axis=3, concat_axis=2, tiled=True)
    in_time = contract("fn,sfbc->snbc", cos_first, regrouped[0]) - contract(
        "fn,sfbc->snbc", sin_first, regrouped[1]
    )
    in_time = in_time * (1.0 / modulus)
    restored = lax.all_to_all(in_time, "context", split_axis=1, concat_axis=2, tiled=True)
    input_grad = restored[0].astype(jnp.bfloat16)
    filter_grad = lax.psum(restored[1, 0], "dp")
    return (input_grad, filter_grad)


def any_body(n_ctx, n_dp, grad_out, inputs, filt):
    n, width = filt.shape
    tile = 32
    fits = (
        n_ctx == 2
        and grad_out.shape[0] == 1
        and n_dp % 2 == 0
        and n % 256 == 0
        and width % (n_ctx * n_dp * tile) == 0
        and width % (n_ctx * 128) == 0
        and 16 * n * (n + width) * 4 <= 40 * 1024 * 1024
    )
    if fits:
        return fused_body(n_ctx, n_dp, grad_out, inputs, filt)
    return body(grad_out, inputs, filt)


def solution(mesh):
    return jax.shard_map(
        functools.partial(any_body, mesh.shape["context"], mesh.shape["dp"]),
        mesh=mesh,
        in_specs=(
            P("dp", "context", "tensor"),
            P("dp", "context", "tensor"),
            P("context", "tensor"),
        ),
        out_specs=(P("dp", "context", "tensor"), P("context", "tensor")),
        check_vma=False,
    )
```
